32 devices in a mesh: dp: 8 (over z, y), tp: 4 (over x, core).
Axes of the slice: x: 2, y: 2, z: 4, core: 2. Of those that a mesh axis runs over, the one named last changes fastest.
Arguments:
- watch_ids: int32 [4096, 50], P(('dp', 'tp')), may hold values from 0 to 131071, as said below
- watch_len: int32 [4096], P(('dp', 'tp')), may hold values from 1 to 50
- search_ids: int32 [4096, 50], P(('dp', 'tp')), may hold values from 0 to 131071, as said below
- search_len: int32 [4096], P(('dp', 'tp')), may hold values from 1 to 50
- search_mask: int32 [4096], P(('dp', 'tp')), may hold values 0 or 1
- positive_ids: int32 [4096], P(('dp', 'tp')), may hold values from 0 to 131071, as said below
- logq_pos: float32 [4096], P(('dp', 'tp')), may hold values from -12 to -9
- negative_ids: int32 [5000], replicated, may hold values from 0 to 131071
- logq_neg: float32 [5000], replicated, may hold values from -12 to -9
- dense_feats: float32 [4096, 128], P(('dp', 'tp')), may hold values from -6 to 6
- watch_table: float32 [131072, 256], P(('dp', 'tp')), may hold values from -6 to 6
- search_table: float32 [131072, 256], P(('dp', 'tp')), may hold values from -6 to 6
- out_table: float32 [131072, 256], P(('dp', 'tp')), may hold values from -0.9 to 0.9
- weight_one: float32 [640, 1024], P(None, 'tp'), may hold values from -0.25 to 0.25
- bias_one: float32 [1024], P('tp'), may hold values from -3 to 3
- weight_two: float32 [1024, 512], P(None, 'tp'), may hold values from -0.1875 to 0.1875
- bias_two: float32 [512], P('tp'), may hold values from -3 to 3
- weight_three: float32 [512, 256], replicated, may hold values from -0.25 to 0.25
- bias_three: float32 [256], replicated, may hold values from -3 to 3
Outputs:
- mean_loss: float32 [], replicated
- watch_grad: float32 [131072, 256], P(('dp', 'tp'))
- search_grad: float32 [131072, 256], P(('dp', 'tp'))
- output_grad: float32 [131072, 256], P(('dp', 'tp'))
- weight_one_grad: float32 [640, 1024], P(None, 'tp')
- bias_one_grad: float32 [1024], P('tp')
- weight_two_grad: float32 [1024, 512], P(None, 'tp')
- bias_two_grad: float32 [512], P('tp')
- weight_three_grad: float32 [512, 256], replicated
- bias_three_grad: float32 [256], replicated
- dense_grad: float32 [4096, 128], P(('dp', 'tp'))
The draws below stay inside these ranges and needn't reach their ends.
Inputs may be any that keep to these rules, and one draw needn't show every extreme that they name: `watch_ids`: the table has 32 shards; shard s owns rows [s * 4096, (s + 1) * 4096), with 4096 = 4096. Of the 6400 ids in the rows of one index of dp+tp, at most 300 = max(2, 300) lie in one shard, and some shard holds exactly 300 of them. `search_ids`: the table has 32 shards; shard s owns rows [s * 4096, (s + 1) * 4096), with 4096 = 4096. Of the 6400 ids in the rows of one index of dp+tp, at most 300 = max(2, 300) lie in one shard, and some shard holds exactly 300 of them. `positive_ids`: the table has 32 shards; shard s owns rows [s * 4096, (s + 1) * 4096), with 4096 = 4096. Of the 128 ids of one index of dp+tp, at most 6 = max(2, 6) lie in one shard, and some shard holds exactly 6 of them.
All inputs are finite; a program needn't handle non-finite values. No bound on the sum of `search_mask` on one device may be relied on, other than what follows from the above.
Results may differ from the reference program's by a relative error of at most 0.0003.
Values sent between devices are 32-bit elements; how exact they have to be, the bound alone decides.
No kernel may reach another device: no remote copies, remote signals or barrier semaphores. Data moves between devices by JAX's collectives and lax.ppermute only.
A program may use at most 192 MiB of HBM per device.

```python
import jax
import jax.numpy as jnp
from jax import lax

E = 256
H1 = 1024
H2 = 512
DENSE = 128
BAG = 50
NEG = 5000
ROWS_DEV = 4096
F = 640
USERS_DEV = 128
SHARDS = 32
USERS = 4096
VOCAB = 131072
CAP = 300
CAPP = 6


def owned_block(key, count, bound):
    keys = jax.random.split(key, 4)
    first = jax.random.randint(keys[0], (), 0, SHARDS).astype(jnp.int32)
    others = jnp.arange(SHARDS - 1, dtype=jnp.int32)
    others = others + (others >= first).astype(jnp.int32)
    pool = jax.random.permutation(keys[1], jnp.repeat(others, bound))[:count - bound]
    owners = jnp.concatenate([jnp.full((bound,), first, jnp.int32), pool])
    owners = jax.random.permutation(keys[2], owners)
    offsets = jax.random.randint(keys[3], (count,), 0, ROWS_DEV).astype(jnp.int32)
    return owners * ROWS_DEV + offsets


def owned_ids(key, count, bound):
    keys = jax.random.split(key, SHARDS)
    return jax.vmap(lambda single: owned_block(single, count, bound))(keys)


def draw_watch_ids(key, part):
    key = jax.random.fold_in(key, 11)
    return owned_ids(key, USERS_DEV * BAG, CAP).reshape(USERS, BAG)


def draw_search_ids(key, part):
    key = jax.random.fold_in(key, 12)
    return owned_ids(key, USERS_DEV * BAG, CAP).reshape(USERS, BAG)


def draw_positive_ids(key, part):
    key = jax.random.fold_in(key, 13)
    return owned_ids(key, USERS_DEV, CAPP).reshape(USERS)


def with_ends(values, rng, smallest, largest):
    longest = values.shape.index(max(values.shape))
    spots = []
    for shift in (0, 1):
        where = [jax.random.randint(jax.random.fold_in(rng, axis), (), 0, length) for axis, length in enumerate(values.shape)]
        where[longest] = (where[longest] + shift) % values.shape[longest]
        spots.append(tuple(where))
    return values.at[spots[0]].set(smallest).at[spots[1]].set(largest)


def steps_of(rng, extent, cuts, least, high):
    def one(dim, shards_of):
        steps = jax.random.uniform(jax.random.fold_in(jax.random.fold_in(rng, 6), dim), (shards_of,), jnp.float32, least / len(cuts), high / len(cuts))
        return jnp.repeat(jnp.exp(steps), extent[dim] // shards_of).reshape((-1,) + (1,) * (len(extent) - dim - 1))

    gain = one(*cuts[0])
    for cut in cuts[1:]:
        gain = gain * one(*cut)
    return gain


def bell_draw(rng, shape, spread, most, cuts=(), kind=jnp.bfloat16):
    values = spread * jax.random.normal(rng, shape, jnp.float32)
    if cuts:
        values = values * steps_of(rng, shape, cuts, -0.22, 0.18)
    return jnp.clip(values, -most, most).astype(kind)


def setup_inputs(seed: int = 0) -> dict:
    key_of = jax.random.split(jax.random.key(seed), 20)
    return {
        "watch_ids": draw_watch_ids(jax.random.fold_in(key_of[19], 71), 0),
        "watch_len": with_ends(jax.random.randint(key_of[1], (USERS,), 1, BAG + 1), jax.random.fold_in(key_of[1], 1), 1, BAG).astype(jnp.int32),
        "search_ids": draw_search_ids(jax.random.fold_in(key_of[19], 71), 0),
        "search_len": with_ends(jax.random.randint(key_of[3], (USERS,), 1, BAG + 1), jax.random.fold_in(key_of[3], 1), 1, BAG).astype(jnp.int32),
        "search_mask": with_ends((jax.random.randint(key_of[4], (USERS,), 0, 4) < 3).astype(jnp.int32), jax.random.fold_in(key_of[4], 1), 0, 1),
        "positive_ids": draw_positive_ids(jax.random.fold_in(key_of[19], 71), 0),
        "logq_pos": jnp.clip(-12.0 + 3.0 * jax.random.uniform(key_of[6], (USERS,), jnp.float32) ** steps_of(key_of[6], (USERS,), ((0, 32),), -0.2, 0.2), -12.0, -9.0),
        "negative_ids": with_ends(jax.random.randint(key_of[7], (NEG,), 0, VOCAB), jax.random.fold_in(key_of[7], 1), 0, VOCAB - 1).astype(jnp.int32),
        "logq_neg": jnp.clip(jax.random.uniform(key_of[8], (NEG,), jnp.float32, -12.0, -9.0), -12.0, -9.0),
        "dense_feats": bell_draw(key_of[9], (USERS, DENSE), 1.0, 6.0, ((0, 32),), jnp.float32),
        "watch_table": bell_draw(key_of[10], (VOCAB, E), 1.0, 6.0, ((0, 32),), jnp.float32),
        "search_table": bell_draw(key_of[11], (VOCAB, E), 1.0, 6.0, ((0, 32),), jnp.float32),
        "out_table": bell_draw(key_of[12], (VOCAB, E), 0.15, 0.9, ((0, 32),), jnp.float32),
        "weight_one": bell_draw(key_of[13], (F, H1), F ** -0.5, 0.25, ((1, 4),), jnp.float32),
        "bias_one": bell_draw(key_of[14], (H1,), 0.5, 3.0, ((0, 4),), jnp.float32),
        "weight_two": bell_draw(key_of[15], (H1, H2), H1 ** -0.5, 0.1875, ((1, 4),), jnp.float32),
        "bias_two": bell_draw(key_of[16], (H2,), 0.5, 3.0, ((0, 4),), jnp.float32),
        "weight_three": bell_draw(key_of[17], (H2, E), H2 ** -0.5, 0.25, (), jnp.float32),
        "bias_three": bell_draw(key_of[18], (E,), 0.5, 3.0, (), jnp.float32),
    }


@jax.custom_vjp
def low(v):
    return lax.optimization_barrier(v.astype(jnp.bfloat16)).astype(jnp.float32)

@jax.custom_vjp
def low_back(v):
    return v

def low_keep(v):
    return (low(v), None)

def low_pass(kept, grad):
    return (grad,)

def back_keep(v):
    return (v, None)

def back_low(kept, grad):
    return (low(grad),)
low.defvjp(low_keep, low_pass)
low_back.defvjp(back_keep, back_low)

def matmul(left, right):
    return jnp.dot(left, right, precision=lax.Precision.HIGHEST, preferred_element_type=jnp.float32)

def pooled(table, ids, lengths):
    valid = (jnp.arange(ids.shape[1])[None, :] < lengths[:, None]).astype(jnp.float32)

    def step(acc, column):
        index, keep = column
        return (acc + table[index] * keep[:, None], None)
    start = jnp.zeros((ids.shape[0], table.shape[1]), jnp.float32)
    acc, unused = lax.scan(step, start, (ids.T, valid.T))
    return acc / lengths.astype(jnp.float32)[:, None]

def reference(watch_ids, watch_len, search_ids, search_len, search_mask, positive_ids, logq_pos, negative_ids, logq_neg, dense_feats, watch_table, search_table, out_table, weight_one, bias_one, weight_two, bias_two, weight_three, bias_three):
    mask_float = search_mask.astype(jnp.float32)

    def forward(wtab, stab, otab, wone, bone, wtwo, btwo, wthree, bthree, dense):
        watch_avg = pooled(wtab, watch_ids, watch_len)
        search_avg = pooled(stab, search_ids, search_len) * mask_float[:, None]
        feats = jnp.concatenate([watch_avg, search_avg, dense], axis=1)
        hidden_a = jax.nn.gelu(matmul(feats, wone) + bone)
        hidden_b = jax.nn.gelu(matmul(hidden_a, wtwo) + btwo)
        user_vec = jax.nn.gelu(matmul(hidden_b, wthree) + bthree)
        pos_rows = otab[positive_ids]
        neg_rows = otab[negative_ids]
        s_pos = lax.optimization_barrier(jnp.sum(user_vec * pos_rows, axis=1)) - logq_pos
        block = min(4096, USERS)
        count = USERS // block
        user_blocks = user_vec.reshape(count, block, E)
        pos_blocks = s_pos.reshape(count, block)

        def block_loss(pair):
            users_here, pos_here = pair
            s_neg = matmul(users_here, neg_rows.T) - logq_neg[None, :]
            scores = jnp.concatenate([pos_here[:, None], s_neg], axis=1)
            top = lax.optimization_barrier(jnp.max(scores, axis=1, keepdims=True))
            lse = top[:, 0] + jnp.log(lax.optimization_barrier(jnp.sum(jnp.exp(scores - top), axis=1)))
            return jnp.sum(lse - pos_here)
        return jnp.sum(lax.map(jax.checkpoint(block_loss), (user_blocks, pos_blocks)))
    total, pull = jax.vjp(forward, watch_table, search_table, out_table, weight_one, bias_one, weight_two, bias_two, weight_three, bias_three, dense_feats)
    grads = pull(jnp.ones((), jnp.float32))
    mean_loss = total / USERS
    return (mean_loss, grads[0], grads[1], grads[2], grads[3], grads[4], grads[5], grads[6], grads[7], grads[8], grads[9])
```

```python
import functools

import jax
import jax.numpy as jnp
from jax import lax
from jax.experimental import pallas as pl
from jax.experimental.pallas import tpu as pltpu
from jax.sharding import PartitionSpec as P

AXES = ("dp", "tp")
F32 = jnp.float32
I32 = jnp.int32
BIG = 1e30
LANES = 128
GROUP = 4
UNROLL = 4
SHIFT = 8
PAD_ROWS = 8


def matmul(left, right):
    return jnp.dot(left, right, precision=lax.Precision.HIGH, preferred_element_type=F32)


def matmul_t(left, right):
    return lax.dot_general(
        left, right, (((1,), (1,)), ((), ())), precision=lax.Precision.HIGH, preferred_element_type=F32
    )


def inner_rows(left, right):
    return lax.dot_general(
        left, right, (((0,), (0,)), ((), ())), precision=lax.Precision.HIGH, preferred_element_type=F32
    )


def swap(x, mask, shards):
    return lax.ppermute(x, AXES, [(i, i ^ mask) for i in range(shards)])


def places(order):
    n = len(order)
    return [sum(((p >> (n - 1 - j)) & 1) << order[j] for j in range(n)) for p in range(1 << n)]


def group_max(cnt_ref, group):
    most = cnt_ref[group * GROUP]
    for k in range(1, GROUP):
        most = jnp.maximum(most, cnt_ref[group * GROUP + k])
    return (most + UNROLL - 1) // UNROLL


def load_indices(idx_ref, group, step, cap):
    base = (group * cap + step * UNROLL) * GROUP
    return [[idx_ref[base + u * GROUP + k] for k in range(GROUP)] for u in range(UNROLL)]


def pool_kernel(groups, users, cap, cnt_ref, idx_ref, tab_ref, send_ref, keep_ref, tab):
    rows = tab_ref.shape[0]
    for h in range(2):
        tab[pl.ds(h, rows, 2), :] = tab_ref[:, h * LANES : (h + 1) * LANES]
    tab[pl.ds(2 * rows, 2 * PAD_ROWS), :] = jnp.zeros((2 * PAD_ROWS, LANES), F32)
    send_ref[...] = jnp.zeros_like(send_ref)
    keep_ref[...] = jnp.zeros_like(keep_ref)
    half = len(groups) // 2
    for place, group in enumerate(groups):
        out = keep_ref if place < half else send_ref
        first = (place % half) * GROUP * users

        def step(i, carry, out=out, first=first, group=group):
            picks = load_indices(idx_ref, group, i, cap)
            source = [[tab[pl.ds(pl.multiple_of((v >> SHIFT) * 2, 2), 2), :] for v in row] for row in picks]
            for u in range(UNROLL):
                where = [first + k * users + (v & ((1 << SHIFT) - 1)) for k, v in enumerate(picks[u])]
                held = [out[w] for w in where]
                for k in range(GROUP):
                    out[where[k]] = held[k] + source[u][k]
            return carry

        lax.fori_loop(0, group_max(cnt_ref, group), step, 0)


def pool(groups, users, cap, counts, index, table):
    rows, width = table.shape
    shards = len(groups) * GROUP
    return pl.pallas_call(
        functools.partial(pool_kernel, groups, users, cap),
        out_shape=[jax.ShapeDtypeStruct((shards // 2 * users, 2, LANES), F32)] * 2,
        in_specs=[pl.BlockSpec(memory_space=pltpu.SMEM)] * 2 + [pl.BlockSpec(memory_space=pltpu.VMEM)],
        out_specs=[pl.BlockSpec(memory_space=pltpu.VMEM)] * 2,
        scratch_shapes=[pltpu.VMEM((2 * (rows + PAD_ROWS), LANES), F32)],
        compiler_params=pltpu.CompilerParams(vmem_limit_bytes=60 << 20),
        cost_estimate=pl.CostEstimate(flops=0, bytes_accessed=40 << 20, transcendentals=0),
    )(counts, index, table)


def spread_kernel(groups, users, cap, cnt_ref, idx_ref, near_ref, far_ref, out_ref, acc):
    rows = out_ref.shape[0]
    acc[...] = jnp.zeros_like(acc)
    half = len(groups) // 2
    for place, group in enumerate(groups):
        source_ref = near_ref if place < half else far_ref
        first = (place % half) * GROUP * users

        def step(i, carry, source_ref=source_ref, first=first, group=group):
            picks = load_indices(idx_ref, group, i, cap)
            source = [
                [source_ref[first + k * users + (v & ((1 << SHIFT) - 1))] for k, v in enumerate(row)]
                for row in picks
            ]
            for u in range(UNROLL):
                for k in range(GROUP):
                    where = pl.ds(pl.multiple_of((picks[u][k] >> SHIFT) * 2, 2), 2)
                    acc[where, :] = acc[where, :] + source[u][k]
            return carry

        lax.fori_loop(0, group_max(cnt_ref, group), step, 0)
    for h in range(2):
        out_ref[:, h * LANES : (h + 1) * LANES] = acc[pl.ds(h, rows, 2), :]


def spread(groups, users, cap, rows, counts, index, near, far):
    width = near.shape[1] * near.shape[2]
    return pl.pallas_call(
        functools.partial(spread_kernel, groups, users, cap),
        out_shape=jax.ShapeDtypeStruct((rows, width), F32),
        in_specs=[pl.BlockSpec(memory_space=pltpu.SMEM)] * 2 + [pl.BlockSpec(memory_space=pltpu.VMEM)] * 2,
        out_specs=pl.BlockSpec(memory_space=pltpu.VMEM),
        scratch_shapes=[pltpu.VMEM((2 * (rows + PAD_ROWS), LANES), F32)],
        compiler_params=pltpu.CompilerParams(vmem_limit_bytes=60 << 20),
        cost_estimate=pl.CostEstimate(flops=0, bytes_accessed=40 << 20, transcendentals=0),
    )(counts, index, near, far)


def shard_counts(owners, shards):
    return jnp.sum((owners[:, None] == jnp.arange(shards, dtype=I32)[None, :]).astype(I32), axis=0)


def fill_owners(owners, shards, cap):
    lack = cap - shard_counts(owners, shards)
    ends = jnp.sum(jnp.tril(jnp.ones((shards, shards), I32)) * lack[None, :], axis=1)
    extra = jnp.arange(shards * cap - owners.shape[0], dtype=I32)
    return jnp.sum((extra[:, None] >= ends[None, :]).astype(I32), axis=1)


def request_keys(table, ids, used, user, users, rows, shards, cap):
    owner = ids // rows
    unit = rows * users
    real = ((table * shards + owner) * 2 + (1 - used)) * unit + (ids % rows) * users + user
    extra = ((table * shards + fill_owners(owner, shards, cap)) * 2 + 1) * unit
    return [real, extra]


def decode_keys(keys, users, rows):
    used = (keys // (rows * users)) % 2 == 0
    return jnp.where(used, (keys // users) % rows, rows), jnp.where(used, keys % users, 0)


def body(
    watch_ids,
    watch_len,
    search_ids,
    search_len,
    search_mask,
    positive_ids,
    logq_pos,
    negative_ids,
    logq_neg,
    dense_feats,
    watch_table,
    search_table,
    out_table,
    weight_one,
    bias_one,
    weight_two,
    bias_two,
    weight_three,
    bias_three,
):
    shards = lax.axis_size(AXES)
    n_tp = lax.axis_size("tp")
    n_dp = shards // n_tp
    mine = lax.axis_index(AXES)
    tp = lax.axis_index("tp")
    dp = lax.axis_index("dp")
    bits = shards.bit_length() - 1
    tp_bits = n_tp.bit_length() - 1
    rows, width = watch_table.shape
    users, bag = watch_ids.shape
    negs = negative_ids.shape[0]
    cap = max(2, 3 * users * bag // (2 * shards))
    cap_pos = max(2, 3 * users // (2 * shards))
    cap_pad = -(-cap // UNROLL) * UNROLL
    order_a = list(range(bits))
    order_b = [0, 2, 1] + list(range(3, bits))
    place_a, place_b = places(order_a), places(order_b)
    groups_a = list(range(shards // GROUP))
    groups_b = [place_a.index(place_b[g * GROUP]) // GROUP for g in groups_a]

    mean = negs / shards
    block = min(-(-negs // 8) * 8, max(8, int(mean + 4.2 * mean**0.5) // 8 * 8))
    neg_owner = negative_ids // rows
    neg_count = shard_counts(neg_owner, shards)
    neg_most = jnp.max(neg_count)
    neg_mine = neg_owner == mine
    own_rows_id, own_logq = lax.sort(
        (jnp.where(neg_mine, negative_ids % rows, rows), logq_neg), num_keys=1
    )
    own_rows_id = jnp.concatenate([own_rows_id, jnp.full((block,), rows, I32)])
    own_logq = jnp.concatenate([own_logq, jnp.full((block,), BIG, F32)])
    first_id = own_rows_id[:block]
    first_logq = jnp.where(first_id < rows, own_logq[:block], 0.0)
    logq_rows = -(-block // (8 * width)) * 8
    own_rows = out_table[jnp.minimum(first_id, rows - 1)]
    payload = jnp.concatenate(
        [own_rows, jnp.pad(first_logq, (0, logq_rows * width - block)).reshape(logq_rows, width)]
    )
    gathered = lax.all_gather(payload, AXES, axis=0, tiled=False)
    neg_rows = gathered.reshape(-1, width)
    neg_real = jnp.arange(block, dtype=I32)[None, :] < neg_count[:, None]
    neg_logq = jnp.where(neg_real, gathered[:, block:, :].reshape(shards, -1)[:, :block], BIG)
    neg_logq = jnp.pad(neg_logq, ((0, 0), (0, logq_rows)), constant_values=BIG).reshape(-1)
    n_all = neg_rows.shape[0]

    w_one = lax.all_gather(weight_one, "tp", axis=1, tiled=True)
    w_two = lax.all_gather(weight_two, "tp", axis=1, tiled=True)
    b_one = lax.all_gather(bias_one, "tp", axis=0, tiled=True)
    b_two = lax.all_gather(bias_two, "tp", axis=0, tiled=True)

    slot = jnp.arange(users * bag, dtype=I32)
    slot_user = slot // bag
    spot = jnp.arange(bag, dtype=I32)[None, :]
    watch_used = (spot < watch_len[:, None]).astype(I32).reshape(-1)
    search_used = ((spot < search_len[:, None]) & (search_mask[:, None] > 0)).astype(I32).reshape(-1)
    user_index = jnp.arange(users, dtype=I32)
    keys = jnp.concatenate(
        request_keys(0, watch_ids.reshape(-1), watch_used, slot_user, users, rows, shards, cap)
        + request_keys(1, search_ids.reshape(-1), search_used, slot_user, users, rows, shards, cap)
        + request_keys(2, positive_ids, 1, user_index, users, rows, shards, cap_pos)
    )
    keys = lax.sort(keys)
    parts = [
        keys[: shards * cap].reshape(shards, cap),
        keys[shards * cap : 2 * shards * cap].reshape(shards, cap),
        keys[2 * shards * cap :].reshape(shards, cap_pos),
    ]
    decoded = [piece for part in parts for piece in decode_keys(part, users, rows)]
    request = jnp.concatenate(decoded, axis=1)
    my_pos_user = jnp.where(decoded[4] < rows, decoded[5], -1)
    asked = lax.all_to_all(
        request.reshape(shards, 1, -1), AXES, split_axis=0, concat_axis=0, tiled=True
    ).reshape(shards, -1)
    pos_row = asked[:, 4 * cap : 4 * cap + cap_pos]
    pos_user = asked[:, 4 * cap + cap_pos :]
    near_first = asked[mine ^ jnp.array(place_a, I32), : 4 * cap]

    def prepared(start):
        row = near_first[:, start : start + cap]
        user = near_first[:, start + cap : start + 2 * cap]
        counts = jnp.sum((row < rows).astype(I32), axis=1)
        packed = jnp.pad(row * (1 << SHIFT) + user, ((0, 0), (0, cap_pad - cap)), constant_values=rows << SHIFT)
        packed = packed.reshape(shards // GROUP, GROUP, cap_pad).transpose(0, 2, 1).reshape(-1)
        return counts, packed

    watch_plan, search_plan = prepared(0), prepared(2 * cap)

    def scatter_sum(order, send, keep):
        total = keep + swap(send, 1 << order[0], shards)
        for b in order[1:]:
            half = total.shape[0] // 2
            total = total[:half] + swap(total[half:], 1 << b, shards)
        return total.reshape(users, width)

    watch_send, watch_keep = pool(groups_a, users, cap_pad, *watch_plan, watch_table)
    search_send, search_keep = pool(groups_b, users, cap_pad, *search_plan, search_table)
    watch_sum = scatter_sum(order_a, watch_send, watch_keep)
    search_sum = scatter_sum(order_b, search_send, search_keep)
    watch_scale = 1.0 / watch_len.astype(F32)[:, None]
    search_scale = search_mask.astype(F32)[:, None] / search_len.astype(F32)[:, None]
    feats = jnp.concatenate([watch_sum * watch_scale, search_sum * search_scale, dense_feats], axis=1)

    served = out_table[jnp.minimum(pos_row, rows - 1)]
    fetched = lax.all_to_all(served, AXES, split_axis=0, concat_axis=0, tiled=True).reshape(-1, width)
    pos_match = my_pos_user.reshape(-1)[None, :] == user_index[:, None]
    pos_slot = jnp.sum(
        jnp.where(pos_match, jnp.arange(shards * cap_pos, dtype=I32)[None, :], 0), axis=1
    )
    pos_rows = fetched[pos_slot]

    def all_negatives(state):
        local = jnp.where(neg_mine[:, None], out_table[negative_ids % rows], 0.0)
        full = lax.psum(local, AXES)
        return (
            jnp.zeros((), I32),
            jnp.pad(full, ((0, max(0, n_all - negs)), (0, 0)))[:n_all],
            jnp.pad(logq_neg, (0, max(0, n_all - negs)), constant_values=BIG)[:n_all],
        )

    overflow = (neg_most > block).astype(I32)
    _, neg_rows, neg_logq = lax.while_loop(
        lambda state: state[0] > 0, all_negatives, (overflow, neg_rows, neg_logq)
    )

    hidden_a, gelu_one = jax.vjp(jax.nn.gelu, matmul(feats, w_one) + b_one)
    hidden_b, gelu_two = jax.vjp(jax.nn.gelu, matmul(hidden_a, w_two) + b_two)
    user_vec, gelu_three = jax.vjp(jax.nn.gelu, matmul(hidden_b, weight_three) + bias_three)

    user_all = lax.all_gather(user_vec, AXES, axis=0, tiled=True)
    s_neg = matmul_t(user_vec, neg_rows) - neg_logq[None, :]
    s_pos = jnp.sum(user_vec * pos_rows, axis=1) - logq_pos
    top = jnp.maximum(jnp.max(s_neg, axis=1), s_pos)
    e_neg = jnp.exp(s_neg - top[:, None])
    e_pos = jnp.exp(s_pos - top)
    totals = jnp.sum(e_neg, axis=1) + e_pos
    lse = top + jnp.log(totals)
    coef = e_pos / totals - 1.0
    g_user = matmul(e_neg, neg_rows) / totals[:, None] + coef[:, None] * pos_rows
    loss_sum = jnp.sum(lse - s_pos)
    stats = lax.all_gather(jnp.stack([lse, coef]), AXES, axis=0, tiled=False)
    lse_all = stats[:, 0].reshape(-1)
    coef_all = stats[:, 1].reshape(-1)

    (g_three,) = gelu_three(g_user)
    (g_two,) = gelu_two(matmul_t(g_three, weight_three))
    (g_one,) = gelu_one(matmul_t(g_two, w_two))
    g_feats = matmul_t(g_one, w_one)
    dense_grad = g_feats[:, 2 * width :]

    def gather_all(order, x):
        x = x.reshape(users, 2, LANES)
        for b in reversed(order[1:]):
            x = jnp.concatenate([x, swap(x, 1 << b, shards)])
        return x, swap(x, 1 << order[0], shards)

    watch_near, watch_far = gather_all(order_a, g_feats[:, :width] * watch_scale)
    search_near, search_far = gather_all(order_b, g_feats[:, width : 2 * width] * search_scale)
    watch_grad = spread(groups_a, users, cap_pad, rows, *watch_plan, watch_near, watch_far)
    search_grad = spread(groups_b, users, cap_pad, rows, *search_plan, search_near, search_far)

    cols_one, cols_two, rows_three = weight_one.shape[1], weight_two.shape[1], weight_three.shape[0] // n_tp
    deep = weight_two.shape[0] // 2
    used_rows = weight_one.shape[0] + deep + rows_three + 4
    n_rows = -(-used_rows // (8 * n_dp)) * 8 * n_dp
    small = jnp.sum(g_three, axis=0)

    def weight_block(j):
        t = tp ^ j
        one = lax.dynamic_slice_in_dim(g_one, t * cols_one, cols_one, 1)
        two = lax.dynamic_slice_in_dim(g_two, t * cols_two, cols_two, 1)
        three = lax.dynamic_slice_in_dim(hidden_b, t * rows_three, rows_three, 1)
        grad_two = inner_rows(hidden_a, two)
        return jnp.concatenate(
            [
                inner_rows(feats, one),
                jnp.concatenate([grad_two[:deep], grad_two[deep:]], axis=1),
                inner_rows(three, g_three),
                jnp.sum(one, axis=0)[None, :],
                jnp.pad(jnp.sum(two, axis=0), (0, width - cols_two))[None, :],
                small[None, :],
                jnp.full((1, width), loss_sum, F32),
                jnp.zeros((n_rows - used_rows, width), F32),
            ]
        )

    blocks = [weight_block(j) for j in range(n_tp)]
    for b in range(tp_bits):
        moved = swap(jnp.concatenate(blocks[1::2]), 1 << b, shards)
        blocks = [
            kept + moved[i * n_rows : (i + 1) * n_rows] for i, kept in enumerate(blocks[0::2])
        ]
    total = blocks[0]
    dp_bits = n_dp.bit_length() - 1
    for b in range(dp_bits):
        half = total.shape[0] // 2
        bit = (dp >> b) & 1
        kept = lax.dynamic_slice_in_dim(total, bit * half, half, 0)
        moved = lax.dynamic_slice_in_dim(total, (1 - bit) * half, half, 0)
        total = kept + swap(moved, 1 << (b + tp_bits), shards)
    for b in reversed(range(dp_bits)):
        bit = (dp >> b) & 1
        other = swap(total, 1 << (b + tp_bits), shards)
        total = jnp.concatenate([jnp.where(bit == 0, total, other), jnp.where(bit == 0, other, total)])
    at = weight_one.shape[0]
    w_one_grad = total[:at]
    w_two_grad = jnp.concatenate([total[at : at + deep, :cols_two], total[at : at + deep, cols_two:]])
    at += deep
    w_three_grad = lax.all_gather(total[at : at + rows_three], "tp", axis=0, tiled=True)
    at += rows_three
    b_one_grad = total[at]
    b_two_grad = total[at + 1, :cols_two]
    b_three_grad = total[at + 2]
    mean_loss = total[at + 3, 0] / F32(users * shards)

    pos_from = (jnp.arange(shards, dtype=I32)[:, None] * users + pos_user).reshape(-1)
    g_pos = user_all[pos_from] * coef_all[pos_from][:, None]
    output_grad = jnp.zeros((rows, width), F32).at[pos_row.reshape(-1)].add(g_pos, mode="drop")

    def add_block(i, grad):
        ids = lax.dynamic_slice_in_dim(own_rows_id, i * block, block, 0)
        logq = lax.dynamic_slice_in_dim(own_logq, i * block, block, 0)
        held = out_table[jnp.minimum(ids, rows - 1)]
        scores = matmul_t(held, user_all) - logq[:, None]
        chance = jnp.exp(jnp.where((ids < rows)[:, None], scores - lse_all[None, :], -BIG))
        return grad.at[ids].add(matmul(chance, user_all), mode="drop")

    my_count = jnp.sum(neg_mine.astype(I32))
    output_grad = lax.fori_loop(0, (my_count + block - 1) // block, add_block, output_grad)
    return (
        mean_loss,
        watch_grad,
        search_grad,
        output_grad,
        w_one_grad,
        b_one_grad,
        w_two_grad,
        b_two_grad,
        w_three_grad,
        b_three_grad,
        dense_grad,
    )


def solution(mesh):
    both = P(AXES)
    rows = P(AXES, None)
    in_specs = (
        rows, both, rows, both, both, both, both, P(), P(), rows, rows, rows, rows,
        P(None, "tp"), P("tp"), P(None, "tp"), P("tp"), P(), P(),
    )
    out_specs = (
        P(), rows, rows, rows, P(None, "tp"), P("tp"), P(None, "tp"), P("tp"), P(), P(), rows,
    )
    return jax.shard_map(body, mesh=mesh, in_specs=in_specs, out_specs=out_specs, check_vma=False)
```

```python
import functools

import jax
import jax.numpy as jnp
from jax import lax
from jax.experimental import pallas as pl
from jax.experimental.pallas import tpu as pltpu
from jax.sharding import PartitionSpec as P

AXES = ("dp", "tp")
F32 = jnp.float32
I32 = jnp.int32
BIG = 1e30
LANES = 128
GROUP = 4
UNROLL = 8
SHIFT = 9
PAD_ROWS = 8
PARTS = 4
PIECES = 4


def matmul(left, right):
    return jnp.dot(left, right, precision=lax.Precision.HIGH, preferred_element_type=F32)


def matmul_t(left, right):
    return lax.dot_general(
        left, right, (((1,), (1,)), ((), ())), precision=lax.Precision.HIGH, preferred_element_type=F32
    )


def inner_rows(left, right):
    return lax.dot_general(
        left, right, (((0,), (0,)), ((), ())), precision=lax.Precision.HIGH, preferred_element_type=F32
    )


def swap(x, mask, shards):
    return lax.ppermute(x, AXES, [(i, i ^ mask) for i in range(shards)])


def after(x, *earlier):
    return lax.optimization_barrier((x, *earlier))[0]


def exchange(moves, shards, beside=()):
    held = lax.optimization_barrier(tuple(x for x, *_ in moves))
    got = tuple(swap(x, sum(1 << b for b in move[1:]), shards) for x, move in zip(held, moves, strict=True))
    return lax.optimization_barrier(got + tuple(beside))


def places(order):
    n = len(order)
    return [sum(((p >> (n - 1 - j)) & 1) << order[j] for j in range(n)) for p in range(1 << n)]


def group_bounds(me_ref, cnt_ref, members, cap):
    owners = [me_ref[0] ^ q for q in members]
    most = cnt_ref[owners[0]]
    for owner in owners[1:]:
        most = jnp.maximum(most, cnt_ref[owner])
    return [owner * cap for owner in owners], (most + UNROLL - 1) // UNROLL


def pool_kernel(places, users, cap, me_ref, cnt_ref, idx_ref, tab_ref, send_ref, keep_ref, tab, raw, sems):
    rows = tab_ref.shape[0]
    part = rows // PARTS
    copies = [
        pltpu.make_async_copy(tab_ref.at[pl.ds(n * part, part)], raw.at[pl.ds(n * part, part)], sems.at[n])
        for n in range(PARTS)
    ]
    for copy in copies:
        copy.start()
    tab[pl.ds(2 * rows, 2 * PAD_ROWS), :] = jnp.zeros((2 * PAD_ROWS, LANES), F32)
    send_ref[...] = jnp.zeros_like(send_ref)
    keep_ref[...] = jnp.zeros_like(keep_ref)
    for n, copy in enumerate(copies):
        copy.wait()
        for h in range(2):
            tab[pl.ds(2 * n * part + h, part, 2), :] = raw[pl.ds(n * part, part), h * LANES : (h + 1) * LANES]
    half = len(places) // 2
    for start in range(0, len(places), GROUP):
        out = keep_ref if start < half else send_ref
        first = (start % half) * 2 * users
        bases, steps = group_bounds(me_ref, cnt_ref, places[start : start + GROUP], cap)

        def step(i, carry, out=out, first=first, bases=bases):
            picks = [[idx_ref[base + (i * UNROLL + u)] for base in bases] for u in range(UNROLL)]
            source = [[tab[pl.ds(pl.multiple_of(v >> SHIFT, 2), 2), :] for v in row] for row in picks]
            for u in range(UNROLL):
                where = [
                    pl.ds(pl.multiple_of(first + k * 2 * users + (v & ((1 << SHIFT) - 1)), 2), 2)
                    for k, v in enumerate(picks[u])
                ]
                held = [out[w, :] for w in where]
                for k in range(GROUP):
                    out[where[k], :] = held[k] + source[u][k]
            return carry

        lax.fori_loop(0, steps, step, 0)


def pool(places, users, cap, me, counts, index, table):
    rows, width = table.shape
    shards = len(places)
    size = 4 * width * (2 * rows + shards * users)
    return pl.pallas_call(
        functools.partial(pool_kernel, places, users, cap),
        out_shape=[jax.ShapeDtypeStruct((shards * users, LANES), F32)] * 2,
        in_specs=[pl.BlockSpec(memory_space=pltpu.SMEM)] * 3 + [pl.BlockSpec(memory_space=pltpu.HBM)],
        out_specs=[pl.BlockSpec(memory_space=pltpu.VMEM)] * 2,
        scratch_shapes=[
            pltpu.VMEM((2 * (rows + PAD_ROWS), LANES), F32),
            pltpu.VMEM((rows, width), F32),
            pltpu.SemaphoreType.DMA((PARTS,)),
        ],
        compiler_params=pltpu.CompilerParams(vmem_limit_bytes=size + (4 << 20)),
        cost_estimate=pl.CostEstimate(flops=0, bytes_accessed=40 << 20, transcendentals=0),
    )(me, counts, index, table)


def spread_kernel(places, users, cap, me_ref, cnt_ref, idx_ref, *refs):
    sources, out_ref, accs = refs[:PIECES], refs[PIECES], refs[PIECES + 1 :]
    rows = out_ref.shape[0]
    for acc in accs:
        acc[...] = jnp.zeros_like(acc)
    piece = len(places) // PIECES
    for start in range(0, len(places), GROUP):
        source_ref = sources[start // piece]
        first = (start % piece) * 2 * users
        bases, steps = group_bounds(me_ref, cnt_ref, places[start : start + GROUP], cap)

        def step(i, carry, source_ref=source_ref, first=first, bases=bases):
            picks = [[idx_ref[base + (i * UNROLL + u)] for base in bases] for u in range(UNROLL)]
            source = [
                [
                    source_ref[pl.ds(pl.multiple_of(first + k * 2 * users + (v & ((1 << SHIFT) - 1)), 2), 2), :]
                    for k, v in enumerate(row)
                ]
                for row in picks
            ]
            for u in range(UNROLL):
                for k in range(0, GROUP, len(accs)):
                    where = [pl.ds(pl.multiple_of(v >> SHIFT, 2), 2) for v in picks[u][k : k + len(accs)]]
                    held = [acc[w, :] for acc, w in zip(accs, where, strict=True)]
                    for n, acc in enumerate(accs):
                        acc[where[n], :] = held[n] + source[u][k + n]
            return carry

        lax.fori_loop(0, steps, step, 0)
    for h in range(2):
        out_ref[:, h * LANES : (h + 1) * LANES] = sum(acc[pl.ds(h, rows, 2), :] for acc in accs)


def spread(places, users, cap, rows, me, counts, index, *sources):
    width = 2 * LANES
    size = 4 * width * (3 * rows + 2 * sources[0].shape[0])
    return pl.pallas_call(
        functools.partial(spread_kernel, places, users, cap),
        out_shape=jax.ShapeDtypeStruct((rows, width), F32),
        in_specs=[pl.BlockSpec(memory_space=pltpu.SMEM)] * 3 + [pl.BlockSpec(memory_space=pltpu.VMEM)] * PIECES,
        out_specs=pl.BlockSpec(memory_space=pltpu.VMEM),
        scratch_shapes=[pltpu.VMEM((2 * (rows + PAD_ROWS), LANES), F32)] * 2,
        compiler_params=pltpu.CompilerParams(vmem_limit_bytes=size + (4 << 20)),
        cost_estimate=pl.CostEstimate(flops=0, bytes_accessed=40 << 20, transcendentals=0),
    )(me, counts, index, *sources)


def split(x):
    high = x.astype(jnp.bfloat16)
    return high, (x - high.astype(F32)).astype(jnp.bfloat16)


def weight_kernel(order, tp_ref, loss_ref, *refs):
    count = (len(refs) - 2) // 2
    out_ref, held, sems = refs[count], refs[count + 1 : -1], refs[-1]
    copies = [pltpu.make_async_copy(refs[n], held[n], sems.at[n]) for n in range(count)]
    for copy in copies:
        copy.start()
    for copy in copies:
        copy.wait()
    f_own, f_rest, a_own, a_rest, b_own, b_rest, grad_ref = held
    n_tp = len(order)
    width = out_ref.shape[1]
    cols_two = grad_ref.shape[2] - 2 * width
    n_feats, n_deep, rows_three = f_own.shape[1], a_own.shape[1] // 2, b_own.shape[1] // n_tp

    def turned(own, rest, lo, size):
        return split(jnp.concatenate([own[:, pl.ds(lo, size)].T, rest[:, pl.ds(lo, size)].T], axis=1))

    def picked(lo, size):
        return split(jnp.concatenate([grad_ref[tp_ref[0] ^ r, :, lo : lo + size] for r in order]))

    def product(left, right):
        (l_high, l_low), (r_high, r_low) = left, right
        return (
            jnp.dot(l_high, r_high, preferred_element_type=F32)
            + jnp.dot(l_low, r_high, preferred_element_type=F32)
            + jnp.dot(l_high, r_low, preferred_element_type=F32)
        )

    one, two, three = picked(0, width), picked(width, cols_two), picked(width + cols_two, width)
    out_ref[:n_feats, :] = product(turned(f_own, f_rest, 0, n_feats), one)
    for h in range(2):
        out_ref[n_feats : n_feats + n_deep, h * cols_two : (h + 1) * cols_two] = product(
            turned(a_own, a_rest, h * n_deep, n_deep), two
        )
    at = n_feats + n_deep
    mine = pl.multiple_of(tp_ref[0] * rows_three, LANES)
    out_ref[at : at + rows_three, :] = product(turned(b_own, b_rest, mine, rows_three), three)
    at += rows_three
    sums = sum(jnp.sum(grad_ref[k], axis=0, keepdims=True) for k in range(n_tp))
    rest = out_ref.shape[0] - at
    out_ref[at:, :] = jnp.concatenate(
        [
            sums[:, :width],
            jnp.concatenate([sums[:, width : width + cols_two], jnp.zeros((1, width - cols_two), F32)], axis=1),
            sums[:, width + cols_two :],
            jnp.full((1, width), loss_ref[0], F32),
            jnp.zeros((rest - 4, width), F32),
        ]
    )


def weight_block(order, n_rows, width, tp, loss, *arrays):
    return pl.pallas_call(
        functools.partial(weight_kernel, order),
        out_shape=jax.ShapeDtypeStruct((n_rows, width), F32),
        in_specs=[pl.BlockSpec(memory_space=pltpu.SMEM)] * 2 + [pl.BlockSpec(memory_space=pltpu.HBM)] * len(arrays),
        out_specs=pl.BlockSpec(memory_space=pltpu.VMEM),
        scratch_shapes=[pltpu.VMEM(x.shape, F32) for x in arrays] + [pltpu.SemaphoreType.DMA((len(arrays),))],
        compiler_params=pltpu.CompilerParams(vmem_limit_bytes=32 << 20),
        cost_estimate=pl.CostEstimate(flops=0, bytes_accessed=16 << 20, transcendentals=0),
    )(tp, loss, *arrays)


def output_kernel(
    users, block, cap_pos, cnt_ref, id_ref, place_ref, logq_ref, pos_ref, pos_user_ref, user_hbm, tab_hbm,
    out_ref, held, logq, acc, user_ref, tab_ref, scaled, sems,
):
    rows = out_ref.shape[0]
    shards = user_ref.shape[0]
    chunk = 4
    tab_copy = pltpu.make_async_copy(tab_hbm, tab_ref, sems.at[0])
    user_copy = pltpu.make_async_copy(user_hbm, user_ref, sems.at[1])
    user_copy.start()
    tab_copy.start()
    out_ref[...] = jnp.zeros_like(out_ref)
    scaled[pl.ds(users, 8), :] = jnp.zeros((8, scaled.shape[1]), F32)
    user_copy.wait()

    def add_pos(s, carry):
        coef = jnp.broadcast_to(user_ref[s, pl.ds(users, 1), users : 2 * users], (LANES, users)).T
        for h in range(scaled.shape[1] // LANES):
            scaled[:users, h * LANES : (h + 1) * LANES] = user_ref[s, :users, h * LANES : (h + 1) * LANES] * coef
        for k in range(cap_pos):
            row = pos_ref[s * cap_pos + k]
            source = jnp.where(row < rows, pos_user_ref[s * cap_pos + k], users)
            at = pl.ds(jnp.minimum(row, rows - 1), 1)
            out_ref[at, :] = out_ref[at, :] + scaled[pl.ds(source, 1), :]
        return carry

    lax.fori_loop(0, shards, add_pos, 0)
    tab_copy.wait()
    count = cnt_ref[0]

    def add_block(r, carry):
        base = r * block

        def fetch(k, carry):
            row = id_ref[base + k]
            held[pl.ds(k, 1), :] = tab_ref[pl.ds(jnp.minimum(row, rows - 1), 1), :]
            q = jnp.where(row < rows, logq_ref[place_ref[base + k]], F32(BIG))
            logq[pl.ds(k, 1), :] = jnp.full((1, LANES), q, F32)
            return carry

        lax.fori_loop(0, block, fetch, 0, unroll=8)
        acc[...] = jnp.zeros_like(acc)
        held_high, held_low = split(held[...])

        def over_users(c, carry):
            parts = [user_ref[c * chunk + j, :users, :] for j in range(chunk)]
            lse = jnp.concatenate(
                [user_ref[c * chunk + j, pl.ds(users, 1), :users] for j in range(chunk)], axis=1
            )
            high, low = split(jnp.concatenate(parts))
            nt = (((1,), (1,)), ((), ()))
            score = (
                lax.dot_general(held_high, high, nt, preferred_element_type=F32)
                + lax.dot_general(held_low, high, nt, preferred_element_type=F32)
                + lax.dot_general(held_high, low, nt, preferred_element_type=F32)
            )
            q = jnp.concatenate([logq[...]] * (chunk * users // LANES), axis=1)
            p_high, p_low = split(jnp.exp(score - q - lse))
            acc[...] += (
                jnp.dot(p_high, high, preferred_element_type=F32)
                + jnp.dot(p_low, high, preferred_element_type=F32)
                + jnp.dot(p_high, low, preferred_element_type=F32)
            )
            return carry

        lax.fori_loop(0, shards // chunk, over_users, 0)

        def put(k, carry):
            at = pl.ds(id_ref[base + k], 1)
            out_ref[at, :] = out_ref[at, :] + acc[pl.ds(k, 1), :]
            return carry

        lax.fori_loop(0, jnp.minimum(block, count - base), put, 0)
        return carry

    lax.fori_loop(0, (count + block - 1) // block, add_block, 0)


def output_rows(users, block, cap_pos, count, ids, places, logq_neg, pos_row, pos_user, user_rows, table):
    rows, width = table.shape
    size = 4 * (2 * rows * width + user_rows.size + 4 * block * width)
    return pl.pallas_call(
        functools.partial(output_kernel, users, block, cap_pos),
        out_shape=jax.ShapeDtypeStruct((rows, width), F32),
        in_specs=[pl.BlockSpec(memory_space=pltpu.SMEM)] * 6 + [pl.BlockSpec(memory_space=pltpu.HBM)] * 2,
        out_specs=pl.BlockSpec(memory_space=pltpu.VMEM),
        scratch_shapes=[
            pltpu.VMEM((block, width), F32),
            pltpu.VMEM((block, LANES), F32),
            pltpu.VMEM((block, width), F32),
            pltpu.VMEM(user_rows.shape, F32),
            pltpu.VMEM(table.shape, F32),
            pltpu.VMEM((users + 8, width), F32),
            pltpu.SemaphoreType.DMA((2,)),
        ],
        compiler_params=pltpu.CompilerParams(vmem_limit_bytes=size + (8 << 20)),
        cost_estimate=pl.CostEstimate(flops=0, bytes_accessed=40 << 20, transcendentals=0),
    )(count, ids, places, logq_neg, pos_row, pos_user, user_rows, table)


def shard_counts(owners, shards):
    return jnp.sum((owners[:, None] == jnp.arange(shards, dtype=I32)[None, :]).astype(I32), axis=0)


def fill_owners(owners, shards, cap):
    lack = cap - shard_counts(owners, shards)
    ends = jnp.sum(jnp.where(jnp.tri(shards, dtype=jnp.bool_), lack[None, :], 0), axis=1)
    extra = jnp.arange(shards * cap - owners.shape[0], dtype=I32)
    return jnp.sum((extra[:, None] >= ends[None, :]).astype(I32), axis=1)


def request_keys(table, ids, used, user, users, rows, shards, cap):
    owner = lax.div(ids, I32(rows))
    unit = rows * users
    real = ((table * shards + owner) * 2 + (1 - used)) * unit + lax.rem(ids, I32(rows)) * users + user
    extra = ((table * shards + fill_owners(owner, shards, cap)) * 2 + 1) * unit
    return [real, extra]


def decode_keys(keys, users, rows):
    used = lax.rem(lax.div(keys, I32(rows * users)), I32(2)) == 0
    row = lax.rem(lax.div(keys, I32(users)), I32(rows))
    return jnp.where(used, row, rows), jnp.where(used, lax.rem(keys, I32(users)), 0)


def body(
    watch_ids,
    watch_len,
    search_ids,
    search_len,
    search_mask,
    positive_ids,
    logq_pos,
    negative_ids,
    logq_neg,
    dense_feats,
    watch_table,
    search_table,
    out_table,
    weight_one,
    bias_one,
    weight_two,
    bias_two,
    weight_three,
    bias_three,
):
    shards = lax.axis_size(AXES)
    n_tp = lax.axis_size("tp")
    n_dp = shards // n_tp
    mine = lax.axis_index(AXES)
    tp = lax.axis_index("tp")
    dp = lax.axis_index("dp")
    bits = shards.bit_length() - 1
    tp_bits = n_tp.bit_length() - 1
    rows, width = watch_table.shape
    users, bag = watch_ids.shape
    negs = negative_ids.shape[0]
    cap = max(2, 3 * users * bag // (2 * shards))
    cap_pos = max(2, 3 * users // (2 * shards))
    cap_pad = -(-cap // UNROLL) * UNROLL
    order_a = list(range(bits))
    order_b = [0, 2, 1] + list(range(3, bits))
    place_a, place_b = places(order_a), places(order_b)
    me = mine.astype(I32).reshape(1)

    neg_owner = lax.div(negative_ids, I32(rows))
    neg_mine = neg_owner == mine
    neg_local = lax.rem(negative_ids, I32(rows))
    neg_span = 1 << (negs - 1).bit_length()
    mean = negs / shards
    block = min(-(-negs // 8) * 8, max(8, int(mean + 4.2 * mean**0.5) // 8 * 8))
    neg_keys = lax.sort(jnp.where(neg_mine, neg_local, rows) * neg_span + jnp.arange(negs, dtype=I32))
    own_rows_id = jnp.pad(lax.div(neg_keys, I32(neg_span)), (0, block), constant_values=rows)
    own_place = jnp.pad(lax.rem(neg_keys, I32(neg_span)), (0, block))
    first_id = own_rows_id[:block]
    first_logq = logq_neg[own_place[:block]]
    logq_rows = -(-block // (8 * width)) * 8
    payload = jnp.concatenate(
        [
            out_table[jnp.minimum(first_id, rows - 1)],
            jnp.pad(first_logq, (0, logq_rows * width - block)).reshape(logq_rows, width),
        ]
    )
    side_bit = tp_bits - 1
    side = (mine >> side_bit) & 1
    side_order = [b for b in reversed(range(bits)) if b != side_bit]
    side_places = jnp.array(
        [sum(((p >> k) & 1) << b for k, b in enumerate(side_order)) for p in range(1 << len(side_order))], I32
    )

    n_feats, cols_two = weight_one.shape[0], weight_two.shape[1]
    bias_pad = 8
    bias_rows = jnp.stack([bias_one, jnp.pad(bias_two, (0, width - cols_two))])
    w_one = jnp.concatenate([weight_one, jnp.pad(bias_rows, ((0, bias_pad - 2), (0, 0)))])
    w_one = lax.all_gather(w_one, "tp", axis=1, tiled=True)
    w_two = lax.all_gather(weight_two, "tp", axis=1, tiled=True)
    deep = weight_two.shape[0] // 2

    slot = jnp.arange(users * bag, dtype=I32)
    slot_user = lax.div(slot, I32(bag))
    spot = jnp.arange(bag, dtype=I32)[None, :]
    watch_used = (spot < watch_len[:, None]).astype(I32).reshape(-1)
    search_used = ((spot < search_len[:, None]) & (search_mask[:, None] > 0)).astype(I32).reshape(-1)
    user_index = jnp.arange(users, dtype=I32)
    keys = jnp.concatenate(
        request_keys(0, watch_ids.reshape(-1), watch_used, slot_user, users, rows, shards, cap)
        + request_keys(1, search_ids.reshape(-1), search_used, slot_user, users, rows, shards, cap)
        + request_keys(2, positive_ids, 1, user_index, users, rows, shards, cap_pos)
    )
    keys, payload = lax.optimization_barrier((keys, payload))
    moved, keys, w_one = exchange([(payload, side_order[0])], shards, [lax.sort(keys), w_one])
    b_one = w_one[n_feats]
    b_two = w_one[n_feats + 1].reshape(n_tp, width)[:, :cols_two].reshape(-1)
    side_rows = jnp.concatenate([payload, moved])
    ends = [shards * cap, 2 * shards * cap, shards * (2 * cap + cap_pos)]
    parts = [
        keys[: ends[0]].reshape(shards, cap),
        keys[ends[0] : ends[1]].reshape(shards, cap),
        keys[ends[1] : ends[2]].reshape(shards, cap_pos),
    ]
    decoded = [piece for part in parts for piece in decode_keys(part, users, rows)]
    request = jnp.concatenate(decoded, axis=1)
    my_pos_user = jnp.where(decoded[4] < rows, decoded[5], -1)
    request, side_rows = lax.optimization_barrier((request.reshape(shards, 1, -1), side_rows))
    asked = lax.all_to_all(request, AXES, split_axis=0, concat_axis=0, tiled=True)
    moved, asked, w_two = exchange([(side_rows, side_order[1])], shards, [asked, w_two])
    side_rows = jnp.concatenate([side_rows, moved])
    asked = asked.reshape(shards, -1)
    for b in side_order[2:-2]:
        (moved,) = exchange([(side_rows, b)], shards)
        side_rows = jnp.concatenate([side_rows, moved])
    pos_row = asked[:, 4 * cap : 4 * cap + cap_pos]
    pos_user = asked[:, 4 * cap + cap_pos :]

    def prepared(start):
        row = asked[:, start : start + cap]
        user = asked[:, start + cap : start + 2 * cap]
        counts = jnp.sum((row < rows).astype(I32), axis=1)
        packed = 2 * row * (1 << SHIFT) + 2 * user
        packed = jnp.pad(packed, ((0, 0), (0, cap_pad - cap)), constant_values=2 * rows << SHIFT)
        return counts, packed.reshape(-1)

    watch_plan, search_plan = prepared(0), prepared(2 * cap)

    neg_count = shard_counts(neg_owner, shards)
    neg_most = jnp.max(neg_count)
    side_half = side_rows.shape[0] // 2
    side_parts = side_rows[:side_half], side_rows[side_half:]
    watch_counts, first_part = lax.optimization_barrier((watch_plan[0], side_parts[0]))
    send, watch_keep = pool(place_a, users, cap_pad, me, watch_counts, watch_plan[1], watch_table)
    first_got, send, watch_keep = exchange([(first_part, side_order[-2])], shards, [send, watch_keep])
    send, search_counts, second_part = lax.optimization_barrier((send, search_plan[0], side_parts[1]))
    search_send, search_keep = pool(place_b, users, cap_pad, me, search_counts, search_plan[1], search_table)
    watch_got, second_got, search_send, search_keep = exchange(
        [(send, order_a[0]), (second_part, side_order[-2])], shards, [search_send, search_keep]
    )
    side_rows = jnp.concatenate([side_rows, first_got, second_got])

    def cut(keep, got):
        half = keep.shape[0] // 2
        return keep[:half] + got[:half], keep[half:] + got[half:]

    (search_got,) = exchange([(search_send, order_b[0])], shards)
    for i in range(1, bits):
        watch_keep, watch_move = cut(watch_keep, watch_got)
        search_keep, search_move = cut(search_keep, search_got)
        moves = [(watch_move, order_a[i]), (search_move, order_b[i])]
        if i == 1:
            watch_move, search_move, side_rows = lax.optimization_barrier((watch_move, search_move, side_rows))
            served = out_table[jnp.minimum(pos_row, rows - 1)]
            fetched = lax.all_to_all(served, AXES, split_axis=0, concat_axis=0, tiled=True)
            side_got = swap(side_rows, 1 << side_order[-1], shards)
            watch_got, search_got, fetched, side_got = exchange(
                [(watch_move, order_a[i]), (search_move, order_b[i])], shards, [fetched, side_got]
            )
        else:
            watch_got, search_got = exchange(moves, shards)
    fetched = fetched.reshape(-1, width)
    watch_sum = watch_keep + watch_got
    search_sum = search_keep + search_got

    neg_rows = jnp.concatenate([side_rows, side_got])
    n_all = neg_rows.shape[0]
    gathered = neg_rows.reshape(-1, payload.shape[0], width)
    neg_count = shard_counts(neg_owner, shards)
    neg_most = jnp.max(neg_count)
    side_count = neg_count[mine ^ side_places]
    neg_real = jnp.arange(block, dtype=I32)[None, :] < side_count[:, None]
    neg_logq = gathered[:, block:, :].reshape(gathered.shape[0], -1)[:, :block]
    neg_logq = jnp.where(neg_real, neg_logq, BIG)
    neg_logq = jnp.pad(neg_logq, ((0, 0), (0, logq_rows)), constant_values=BIG).reshape(-1)

    watch_sum = watch_sum.reshape(users, width)
    search_sum = search_sum.reshape(users, width)
    watch_scale = 1.0 / watch_len.astype(F32)[:, None]
    search_scale = search_mask.astype(F32)[:, None] / search_len.astype(F32)[:, None]
    feats = jnp.concatenate([watch_sum * watch_scale, search_sum * search_scale, dense_feats], axis=1)

    def first_layer(x):
        return matmul(jnp.pad(x, ((0, 0), (0, bias_pad))), w_one) + b_one


    pos_match = my_pos_user.reshape(-1)[None, :] == user_index[:, None]
    pos_slot = jnp.sum(
        jnp.where(pos_match, jnp.arange(shards * cap_pos, dtype=I32)[None, :], 0), axis=1
    )
    pos_rows = fetched[pos_slot]

    neg_half = -(-negs // 2)
    assert neg_half <= n_all

    def all_negatives(state):
        local = jnp.where(neg_mine[:, None], out_table[neg_local], 0.0)
        full = jnp.pad(lax.psum(local, AXES), ((0, 2 * neg_half - negs), (0, 0)))
        logq = jnp.pad(logq_neg, (0, 2 * neg_half - negs), constant_values=BIG)
        return (
            jnp.zeros((), I32),
            jnp.pad(lax.dynamic_slice_in_dim(full, side * neg_half, neg_half), ((0, n_all - neg_half), (0, 0))),
            jnp.pad(
                lax.dynamic_slice_in_dim(logq, side * neg_half, neg_half), (0, n_all - neg_half), constant_values=BIG
            ),
        )

    overflow = (neg_most > block).astype(I32)
    _, neg_rows, neg_logq = lax.while_loop(
        lambda state: state[0] > 0, all_negatives, (overflow, neg_rows, neg_logq)
    )

    hidden_a, gelu_one = jax.vjp(jax.nn.gelu, first_layer(feats))
    hidden_b, gelu_two = jax.vjp(jax.nn.gelu, matmul(hidden_a, w_two) + b_two)
    user_vec, gelu_three = jax.vjp(jax.nn.gelu, matmul(hidden_b, weight_three) + bias_three)

    def side_sums(vectors):
        score = matmul_t(vectors, neg_rows) - neg_logq[None, :]
        top = jnp.max(score, axis=1)
        weight = jnp.exp(score - top[:, None])
        return matmul(weight, neg_rows), top, jnp.sum(weight, axis=1)

    partner_vec = swap(user_vec, 1 << side_bit, shards)
    g_here, top_here, sum_here = side_sums(user_vec)
    g_sent, top_sent, sum_sent = side_sums(partner_vec)
    sent = jnp.concatenate(
        [g_sent, jnp.pad(jnp.concatenate([top_sent, sum_sent])[None, :], ((0, 7), (0, width - 2 * users)))]
    )
    got = swap(sent, 1 << side_bit, shards)
    g_there, top_there, sum_there = got[:users], got[users, :users], got[users, users : 2 * users]
    s_pos = jnp.sum(user_vec * pos_rows, axis=1) - logq_pos
    top = jnp.maximum(jnp.maximum(top_here, top_there), s_pos)
    scale_here, scale_there, e_pos = jnp.exp(top_here - top), jnp.exp(top_there - top), jnp.exp(s_pos - top)
    totals = sum_here * scale_here + sum_there * scale_there + e_pos
    lse = top + jnp.log(totals)
    coef = e_pos / totals - 1.0
    g_user = (
        g_here * (scale_here / totals)[:, None]
        + g_there * (scale_there / totals)[:, None]
        + coef[:, None] * pos_rows
    )
    loss_sum = jnp.sum(lse - s_pos)
    user_rows = jnp.concatenate(
        [user_vec, jnp.pad(jnp.concatenate([lse, coef])[None, :], ((0, 7), (0, width - 2 * users)))]
    )

    user_rows = lax.all_gather(user_rows, AXES, axis=0, tiled=False)

    (g_three,) = gelu_three(g_user)
    (g_two,) = gelu_two(matmul_t(g_three, weight_three))
    (g_one,) = gelu_one(matmul_t(g_two, w_two))
    feats_held = after(feats, got)
    g_feats = matmul_t(g_one, w_one)[:, :n_feats]
    dense_grad = g_feats[:, 2 * width :]
    moved, g_feats = exchange([(feats_held, side_bit)], shards, [g_feats])
    feats_group = jnp.concatenate([feats, moved])
    group_order = [0, 1 << side_bit]

    watch_out = (g_feats[:, :width] * watch_scale).reshape(2 * users, LANES)
    search_out = (g_feats[:, width : 2 * width] * search_scale).reshape(2 * users, LANES)
    rows_three = weight_three.shape[0] // n_tp
    used_rows = weight_one.shape[0] + deep + rows_three + 4
    n_rows = -(-used_rows // (8 * n_dp)) * 8 * n_dp
    grads = jnp.stack(
        [
            jnp.concatenate(
                [
                    g_one[:, t * width : (t + 1) * width],
                    g_two[:, t * cols_two : (t + 1) * cols_two],
                    g_three,
                ],
                axis=1,
            )
            for t in range(n_tp)
        ]
    )
    dp_order = [*range(tp_bits + 1, bits), tp_bits]

    def halves(total, b):
        bit = (mine >> b) & 1
        half = total.shape[0] // 2
        return (
            lax.dynamic_slice_in_dim(total, bit * half, half, 0),
            lax.dynamic_slice_in_dim(total, (1 - bit) * half, half, 0),
        )

    def joined(total, other, b):
        bit = (mine >> b) & 1
        return jnp.concatenate([jnp.where(bit == 0, total, other), jnp.where(bit == 0, other, total)])

    watch_out, search_out, grads, feats_group = lax.optimization_barrier((watch_out, search_out, grads, feats_group))
    watch_pieces, search_pieces = [watch_out], [search_out]
    done = 0

    def scatter(total, b):
        kept, moved = halves(total, b)
        return kept, (moved, b)

    for i in reversed(range(1, bits)):
        watch_out, search_out = jnp.concatenate(watch_pieces), jnp.concatenate(search_pieces)
        moves = [(watch_out, order_a[i]), (search_out, order_b[i])]
        if i == bits - 1:
            grads = lax.all_to_all(grads, "tp", split_axis=0, concat_axis=0, tiled=True)
            for b in reversed(range(side_bit)):
                (moved,) = exchange([(feats_group, b)], shards)
                feats_group = jnp.concatenate([feats_group, moved])
                group_order = group_order + [r | 1 << b for r in group_order]
            feats_rest = feats_group[users:]
            a_rest = jax.nn.gelu(first_layer(feats_rest))
            b_rest = jax.nn.gelu(matmul(a_rest, w_two) + b_two)
            watch_got, search_got, a_rest, b_rest = exchange(moves, shards, [a_rest, b_rest])
        elif i == bits - 2:
            watch_got, search_got, grads = exchange(moves, shards, [grads])
            total = weight_block(
                group_order, n_rows, width, tp.astype(I32).reshape(1), loss_sum.reshape(1),
                feats, feats_rest, hidden_a, a_rest, hidden_b, b_rest, grads,
            )
            kept, move = scatter(total, dp_order[0])
            done = 1
        elif i > 1:
            watch_got, search_got, got = exchange(moves + [move], shards)
            kept, move = scatter(kept + got, dp_order[done])
            done += 1
        else:
            watch_out, search_out, first, user_rows = lax.optimization_barrier((watch_out, search_out, move[0], user_rows))
            output_grad = output_rows(
                users, block, cap_pos, jnp.sum(neg_mine.astype(I32)).reshape(1), own_rows_id, own_place, logq_neg,
                pos_row.reshape(-1), pos_user.reshape(-1), user_rows, out_table,
            )
            got, output_grad = exchange([(first, move[1])], shards, [output_grad])
            total = kept + got
            for b in dp_order[done:]:
                kept, move = scatter(total, b)
                (got,) = exchange([move], shards)
                total = kept + got
            watch_got, search_got, total = exchange(
                [(watch_out, order_a[i]), (search_out, order_b[i])], shards, [total]
            )
        watch_pieces, search_pieces = [watch_out, watch_got], [search_out, search_got]

    *far, got = exchange(
        [(x, order_a[0]) for x in watch_pieces] + [(x, order_b[0]) for x in search_pieces] + [(total, dp_order[-1])],
        shards,
    )
    total = joined(total, got, dp_order[-1])
    for b in reversed(dp_order[2:-1]):
        (got,) = exchange([(total, b)], shards)
        total = joined(total, got, b)
    watch_counts, total = lax.optimization_barrier((watch_plan[0], total))
    watch_grad = spread(place_a, users, cap_pad, rows, me, watch_counts, watch_plan[1], *watch_pieces, *far[:2])
    got, watch_grad = exchange([(total, dp_order[1])], shards, [watch_grad])
    total = joined(total, got, dp_order[1])
    search_counts, total = lax.optimization_barrier((search_plan[0], total))
    search_grad = spread(place_b, users, cap_pad, rows, me, search_counts, search_plan[1], *search_pieces, *far[2:])
    got, search_grad = exchange([(total, dp_order[0])], shards, [search_grad])
    total = joined(total, got, dp_order[0])

    at = weight_one.shape[0]
    w_one_grad = total[:at]
    w_two_grad = jnp.concatenate([total[at : at + deep, :cols_two], total[at : at + deep, cols_two:]])
    at += deep
    b_one_grad = total[at + rows_three]
    b_two_grad = total[at + rows_three + 1, :cols_two]
    b_three_grad = total[at + rows_three + 2]
    whole = total[at : at + rows_three + 8]
    others = exchange([(whole, *[b for b in range(tp_bits) if r >> b & 1]) for r in range(1, n_tp)], shards)
    whole = jnp.stack([whole, *others])
    whole = jnp.concatenate([lax.dynamic_slice_in_dim(whole, t ^ tp, 1, 0) for t in range(n_tp)])
    w_three_grad = whole[:, :rows_three].reshape(-1, width)
    mean_loss = jnp.sum(whole[:, rows_three + 3, 0]) / F32(users * shards)
    return (
        mean_loss,
        watch_grad,
        search_grad,
        output_grad,
        w_one_grad,
        b_one_grad,
        w_two_grad,
        b_two_grad,
        w_three_grad,
        b_three_grad,
        dense_grad,
    )


def solution(mesh):
    both = P(AXES)
    rows = P(AXES, None)
    in_specs = (
        rows, both, rows, both, both, both, both, P(), P(), rows, rows, rows, rows,
        P(None, "tp"), P("tp"), P(None, "tp"), P("tp"), P(), P(),
    )
    out_specs = (
        P(), rows, rows, rows, P(None, "tp"), P("tp"), P(None, "tp"), P("tp"), P(), P(), rows,
    )
    return jax.shard_map(body, mesh=mesh, in_specs=in_specs, out_specs=out_specs, check_vma=False)
```

```python
import functools

import jax
import jax.numpy as jnp
from jax import lax
from jax.experimental import pallas as pl
from jax.experimental.pallas import tpu as pltpu
from jax.sharding import PartitionSpec as P

AXES = ("dp", "tp")
F32 = jnp.float32
I32 = jnp.int32
BIG = 1e30
LANES = 128
GROUP = 4
UNROLL = 8
SHIFT = 9
PAD_ROWS = 8
PARTS = 4
PIECES = 4


def matmul(left, right):
    return jnp.dot(left, right, precision=lax.Precision.HIGH, preferred_element_type=F32)


def matmul_t(left, right):
    return lax.dot_general(
        left, right, (((1,), (1,)), ((), ())), precision=lax.Precision.HIGH, preferred_element_type=F32
    )


def inner_rows(left, right):
    return lax.dot_general(
        left, right, (((0,), (0,)), ((), ())), precision=lax.Precision.HIGH, preferred_element_type=F32
    )


def swap(x, mask, shards):
    return lax.ppermute(x, AXES, [(i, i ^ mask) for i in range(shards)])


def after(x, *earlier):
    return lax.optimization_barrier((x, *earlier))[0]


def exchange(moves, shards, beside=()):
    held = lax.optimization_barrier(tuple(x for x, *_ in moves))
    got = tuple(swap(x, sum(1 << b for b in move[1:]), shards) for x, move in zip(held, moves, strict=True))
    return lax.optimization_barrier(got + tuple(beside))


def places(order):
    n = len(order)
    return [sum(((p >> (n - 1 - j)) & 1) << order[j] for j in range(n)) for p in range(1 << n)]


def group_bounds(me_ref, cnt_ref, members, cap):
    owners = [me_ref[0] ^ q for q in members]
    most = cnt_ref[owners[0]]
    for owner in owners[1:]:
        most = jnp.maximum(most, cnt_ref[owner])
    return [owner * cap for owner in owners], (most + UNROLL - 1) // UNROLL


def pool_kernel(places, users, cap, me_ref, cnt_ref, idx_ref, tab_ref, send_ref, keep_ref, tab, raw, sems):
    rows = tab_ref.shape[0]
    part = rows // PARTS
    copies = [
        pltpu.make_async_copy(tab_ref.at[pl.ds(n * part, part)], raw.at[pl.ds(n * part, part)], sems.at[n])
        for n in range(PARTS)
    ]
    for copy in copies:
        copy.start()
    tab[pl.ds(2 * rows, 2 * PAD_ROWS), :] = jnp.zeros((2 * PAD_ROWS, LANES), F32)
    send_ref[...] = jnp.zeros_like(send_ref)
    keep_ref[...] = jnp.zeros_like(keep_ref)
    for n, copy in enumerate(copies):
        copy.wait()
        for h in range(2):
            tab[pl.ds(2 * n * part + h, part, 2), :] = raw[pl.ds(n * part, part), h * LANES : (h + 1) * LANES]
    half = len(places) // 2
    for start in range(0, len(places), GROUP):
        out = keep_ref if start < half else send_ref
        first = (start % half) * 2 * users
        bases, steps = group_bounds(me_ref, cnt_ref, places[start : start + GROUP], cap)

        def step(i, carry, out=out, first=first, bases=bases):
            picks = [[idx_ref[base + (i * UNROLL + u)] for base in bases] for u in range(UNROLL)]
            source = [[tab[pl.ds(pl.multiple_of(v >> SHIFT, 2), 2), :] for v in row] for row in picks]
            for u in range(UNROLL):
                where = [
                    pl.ds(pl.multiple_of(first + k * 2 * users + (v & ((1 << SHIFT) - 1)), 2), 2)
                    for k, v in enumerate(picks[u])
                ]
                held = [out[w, :] for w in where]
                for k in range(GROUP):
                    out[where[k], :] = held[k] + source[u][k]
            return carry

        lax.fori_loop(0, steps, step, 0)


def pool(places, users, cap, me, counts, index, table):
    rows, width = table.shape
    shards = len(places)
    return pl.pallas_call(
        functools.partial(pool_kernel, places, users, cap),
        out_shape=[jax.ShapeDtypeStruct((shards * users, LANES), F32)] * 2,
        in_specs=[pl.BlockSpec(memory_space=pltpu.SMEM)] * 3 + [pl.BlockSpec(memory_space=pltpu.HBM)],
        out_specs=[pl.BlockSpec(memory_space=pltpu.VMEM)] * 2,
        scratch_shapes=[
            pltpu.VMEM((2 * (rows + PAD_ROWS), LANES), F32),
            pltpu.VMEM((rows, width), F32),
            pltpu.SemaphoreType.DMA((PARTS,)),
        ],
        compiler_params=pltpu.CompilerParams(vmem_limit_bytes=62 << 20),
        cost_estimate=pl.CostEstimate(flops=0, bytes_accessed=40 << 20, transcendentals=0),
    )(me, counts, index, table)


def spread_kernel(places, users, cap, me_ref, cnt_ref, idx_ref, *refs):
    sources, out_ref, accs = refs[:PIECES], refs[PIECES], refs[PIECES + 1 :]
    rows = out_ref.shape[0]
    for acc in accs:
        acc[...] = jnp.zeros_like(acc)
    piece = len(places) // PIECES
    for start in range(0, len(places), GROUP):
        source_ref = sources[start // piece]
        first = (start % piece) * 2 * users
        bases, steps = group_bounds(me_ref, cnt_ref, places[start : start + GROUP], cap)

        def step(i, carry, source_ref=source_ref, first=first, bases=bases):
            picks = [[idx_ref[base + (i * UNROLL + u)] for base in bases] for u in range(UNROLL)]
            source = [
                [
                    source_ref[pl.ds(pl.multiple_of(first + k * 2 * users + (v & ((1 << SHIFT) - 1)), 2), 2), :]
                    for k, v in enumerate(row)
                ]
                for row in picks
            ]
            for u in range(UNROLL):
                for k in range(0, GROUP, len(accs)):
                    where = [pl.ds(pl.multiple_of(v >> SHIFT, 2), 2) for v in picks[u][k : k + len(accs)]]
                    held = [acc[w, :] for acc, w in zip(accs, where, strict=True)]
                    for n, acc in enumerate(accs):
                        acc[where[n], :] = held[n] + source[u][k + n]
            return carry

        lax.fori_loop(0, steps, step, 0)
    for h in range(2):
        out_ref[:, h * LANES : (h + 1) * LANES] = sum(acc[pl.ds(h, rows, 2), :] for acc in accs)


def spread(places, users, cap, rows, me, counts, index, *sources):
    width = 2 * LANES
    size = 4 * width * (3 * rows + 2 * sources[0].shape[0])
    return pl.pallas_call(
        functools.partial(spread_kernel, places, users, cap),
        out_shape=jax.ShapeDtypeStruct((rows, width), F32),
        in_specs=[pl.BlockSpec(memory_space=pltpu.SMEM)] * 3 + [pl.BlockSpec(memory_space=pltpu.VMEM)] * PIECES,
        out_specs=pl.BlockSpec(memory_space=pltpu.VMEM),
        scratch_shapes=[pltpu.VMEM((2 * (rows + PAD_ROWS), LANES), F32)] * 2,
        compiler_params=pltpu.CompilerParams(vmem_limit_bytes=size + (4 << 20)),
        cost_estimate=pl.CostEstimate(flops=0, bytes_accessed=40 << 20, transcendentals=0),
    )(me, counts, index, *sources)


def split(x):
    high = x.astype(jnp.bfloat16)
    return high, (x - high.astype(F32)).astype(jnp.bfloat16)


NN = (((1,), (0,)), ((), ()))
NT = (((1,), (1,)), ((), ()))


def product(left, right, dims):
    (l_high, l_low), (r_high, r_low) = left, right
    one = functools.partial(lax.dot_general, dimension_numbers=dims, preferred_element_type=F32)
    return one(l_high, r_high) + one(l_low, r_high) + one(l_high, r_low)


def down(row):
    return jnp.broadcast_to(row, (LANES, row.shape[1])).T


def side_kernel(vec_ref, *refs):
    out_ref = refs[-1]
    count = (len(refs) - 1) // 2
    parts = [split(r[...]) for r in refs[:count]]
    vectors = split(vec_ref[...])
    scores = [product(vectors, part, NT) - q[...] for part, q in zip(parts, refs[count:-1], strict=True)]
    top = functools.reduce(jnp.maximum, [jnp.max(x, axis=1, keepdims=True) for x in scores])
    weights = [jnp.exp(x - top) for x in scores]
    users, width = vec_ref.shape
    out_ref[:users, :] = sum(product(split(x), part, NN) for x, part in zip(weights, parts, strict=True))
    total = sum(jnp.sum(x, axis=1, keepdims=True) for x in weights)
    across = [jnp.broadcast_to(x, (users, LANES)).T[:8] for x in (top, total)]
    out_ref[users:, :] = jnp.concatenate(across, axis=1)


def side_sums(vectors, parts, logqs):
    users, width = vectors.shape
    return pl.pallas_call(
        side_kernel,
        out_shape=jax.ShapeDtypeStruct((users + 8, width), F32),
        in_specs=[pl.BlockSpec(memory_space=pltpu.VMEM)] * (1 + 2 * len(parts)),
        out_specs=pl.BlockSpec(memory_space=pltpu.VMEM),
        compiler_params=pltpu.CompilerParams(vmem_limit_bytes=32 << 20),
        cost_estimate=pl.CostEstimate(flops=0, bytes_accessed=16 << 20, transcendentals=0),
    )(vectors, *parts, *[q[None, :] for q in logqs])


def gelu(x):
    scale = (2.0 / jnp.pi) ** 0.5
    return 0.5 * x * (1.0 + jnp.tanh(scale * (x + 0.044715 * x * x * x)))


def gelu_slope(x):
    scale = (2.0 / jnp.pi) ** 0.5
    t = jnp.tanh(scale * (x + 0.044715 * x * x * x))
    return 0.5 * (1.0 + t) + 0.5 * x * (1.0 - t * t) * (scale * (1.0 + 3 * 0.044715 * x * x))


def finish_kernel(
    here_ref, there_ref, rows_ref, vec_ref, pos_ref, z1_ref, z2_ref, z3_ref, w1_ref, w2_ref, w3_ref,
    g3_ref, both_ref, dense_ref, loss_ref,
):
    users, width = vec_ref.shape
    halves = [slice(h * LANES, (h + 1) * LANES) for h in range(width // LANES)]
    top_here, sum_here = (down(here_ref[users : users + 1, h]) for h in halves)
    top_there, sum_there = (down(there_ref[users : users + 1, h]) for h in halves)
    logq, watch_scale, search_scale = (down(rows_ref[k : k + 1, :]) for k in range(3))
    s_pos = jnp.sum(vec_ref[...] * pos_ref[...], axis=1, keepdims=True) - logq
    top = jnp.maximum(jnp.maximum(top_here, top_there), s_pos)
    e_here, e_there, e_pos = jnp.exp(top_here - top), jnp.exp(top_there - top), jnp.exp(s_pos - top)
    totals = sum_here * e_here + sum_there * e_there + e_pos
    lse = top + jnp.log(totals)
    coef = e_pos / totals - 1.0
    e_here, e_there = e_here / totals, e_there / totals
    g_user = jnp.concatenate(
        [here_ref[:users, h] * e_here + there_ref[:users, h] * e_there + pos_ref[:, h] * coef for h in halves], axis=1
    )
    loss_ref[...] = jnp.broadcast_to(jnp.sum((lse - s_pos)[:, :1], axis=0, keepdims=True), loss_ref.shape)
    both_ref[4 * users :, :] = jnp.concatenate([lse.T[:1], coef.T[:1], jnp.zeros((6, LANES), F32)])
    g3 = g_user * gelu_slope(z3_ref[...])
    g2 = product(split(g3), split(w3_ref[...]), NT) * gelu_slope(z2_ref[...])
    g1 = product(split(g2), split(w2_ref[...]), NT) * gelu_slope(z1_ref[...])
    g0 = product(split(g1), split(w1_ref[...]), NT)
    g3_ref[...] = g3
    for k, scale in enumerate((watch_scale, search_scale)):
        for h in range(2):
            lanes = slice(k * width + h * LANES, k * width + (h + 1) * LANES)
            both_ref[pl.ds(2 * k * users + h, users, 2), :] = g0[:, lanes] * scale
    dense_ref[...] = g0[:, 2 * width :]


def finish(n_feats, *arrays):
    users, width = arrays[3].shape
    shapes = [(users, width), (4 * users + 8, LANES), (users, n_feats - 2 * width), (8, LANES)]
    return pl.pallas_call(
        finish_kernel,
        out_shape=[jax.ShapeDtypeStruct(x, F32) for x in shapes],
        in_specs=[pl.BlockSpec(memory_space=pltpu.VMEM)] * len(arrays),
        out_specs=[pl.BlockSpec(memory_space=pltpu.VMEM)] * len(shapes),
        compiler_params=pltpu.CompilerParams(vmem_limit_bytes=32 << 20),
        cost_estimate=pl.CostEstimate(flops=0, bytes_accessed=16 << 20, transcendentals=0),
    )(*arrays)


def weight_kernel(tp_ref, loss_ref, *refs):
    count = (len(refs) - 3) // 2
    out_ref, held, g2_ref, sems = refs[count], refs[count + 1 : -2], refs[-2], refs[-1]
    copies = [pltpu.make_async_copy(refs[n], held[n], sems.at[n]) for n in range(count)]
    for copy in copies:
        copy.start()
    for copy in copies:
        copy.wait()
    feats, z1, z2, g3, w2, w3 = held
    width = out_ref.shape[1]
    n_feats, n_deep = feats.shape[1], z1.shape[1] // 2
    n_tp = z1.shape[1] // width
    cols_two = z2.shape[1] // n_tp
    mine_one = pl.ds(pl.multiple_of(tp_ref[0] * width, LANES), width)
    mine_two = pl.ds(pl.multiple_of(tp_ref[0] * cols_two, LANES), cols_two)

    def turned(x):
        return split(x.T)

    three = split(g3[...])
    g2_ref[...] = product(three, split(w3[...]), NT) * gelu_slope(z2[...])
    two = g2_ref[:, mine_two]
    one = product(split(g2_ref[...]), split(w2[mine_one, :]), NT) * gelu_slope(z1[:, mine_one])
    out_ref[:n_feats, :] = product(turned(feats[...]), split(one), NN)
    for h in range(2):
        out_ref[n_feats : n_feats + n_deep, h * cols_two : (h + 1) * cols_two] = product(
            turned(gelu(z1[:, h * n_deep : (h + 1) * n_deep])), split(two), NN
        )
    at = n_feats + n_deep
    out_ref[at : at + cols_two, :] = product(turned(gelu(z2[:, mine_two])), three, NN)
    at += cols_two
    rest = out_ref.shape[0] - at
    out_ref[at:, :] = jnp.concatenate(
        [
            jnp.sum(one, axis=0, keepdims=True),
            jnp.concatenate([jnp.sum(two, axis=0, keepdims=True), jnp.zeros((1, width - cols_two), F32)], axis=1),
            jnp.sum(g3[...], axis=0, keepdims=True),
            jnp.full((1, width), loss_ref[0], F32),
            jnp.zeros((rest - 4, width), F32),
        ]
    )


def weight_block(n_rows, tp, loss, *arrays):
    width = arrays[3].shape[1]
    return pl.pallas_call(
        weight_kernel,
        out_shape=jax.ShapeDtypeStruct((n_rows, width), F32),
        in_specs=[pl.BlockSpec(memory_space=pltpu.SMEM)] * 2 + [pl.BlockSpec(memory_space=pltpu.HBM)] * len(arrays),
        out_specs=pl.BlockSpec(memory_space=pltpu.VMEM),
        scratch_shapes=[pltpu.VMEM(x.shape, F32) for x in (*arrays, arrays[2])]
        + [pltpu.SemaphoreType.DMA((len(arrays),))],
        compiler_params=pltpu.CompilerParams(vmem_limit_bytes=62 << 20),
        cost_estimate=pl.CostEstimate(flops=0, bytes_accessed=16 << 20, transcendentals=0),
    )(tp, loss, *arrays)


def output_kernel(
    users, block, cap_pos, cnt_ref, id_ref, place_ref, logq_ref, pos_ref, pos_user_ref, user_at, coef_ref, lse_ref,
    near_hbm, far_hbm, tab_hbm,
    out_ref, held, logq, acc, user_ref, tab_ref, sems,
):
    rows = out_ref.shape[0]
    shards = user_ref.shape[0]
    chunk = 4
    tab_copy = pltpu.make_async_copy(tab_hbm, tab_ref, sems.at[0])
    half = shards // 2
    user_copies = [
        pltpu.make_async_copy(x, user_ref.at[pl.ds(n * half, half)], sems.at[1 + n])
        for n, x in enumerate((near_hbm, far_hbm))
    ]
    for copy in user_copies:
        copy.start()
    tab_copy.start()
    out_ref[...] = jnp.zeros_like(out_ref)
    for copy in user_copies:
        copy.wait()

    def add_pos(s, carry):
        entries = [(pos_ref[s * cap_pos + k], pos_user_ref[s * cap_pos + k]) for k in range(cap_pos)]
        coefs = [jnp.where(row < rows, coef_ref[user_at[s] * users + user], 0.0) for row, user in entries]
        added = [user_ref[user_at[s], pl.ds(user, 1), :] * c for (_, user), c in zip(entries, coefs, strict=True)]
        for (row, _), x in zip(entries, added, strict=True):
            at = pl.ds(jnp.minimum(row, rows - 1), 1)
            out_ref[at, :] = out_ref[at, :] + x
        return carry

    lax.fori_loop(0, shards, add_pos, 0)
    tab_copy.wait()
    count = cnt_ref[0]

    def add_block(r, carry):
        base = r * block

        def fetch(k, carry):
            row = id_ref[base + k]
            held[pl.ds(k, 1), :] = tab_ref[pl.ds(jnp.minimum(row, rows - 1), 1), :]
            q = jnp.where(row < rows, logq_ref[place_ref[base + k]], F32(BIG))
            logq[pl.ds(k, 1), :] = jnp.full((1, LANES), q, F32)
            return carry

        lax.fori_loop(0, block, fetch, 0, unroll=8)
        acc[...] = jnp.zeros_like(acc)
        held_high, held_low = split(held[...])

        def over_users(c, carry):
            parts = [user_ref[c * chunk + j, :users, :] for j in range(chunk)]
            lse = jnp.concatenate(
                [lse_ref[c * chunk + j, 0:1, :] for j in range(chunk)], axis=1
            )
            high, low = split(jnp.concatenate(parts))
            nt = (((1,), (1,)), ((), ()))
            score = (
                lax.dot_general(held_high, high, nt, preferred_element_type=F32)
                + lax.dot_general(held_low, high, nt, preferred_element_type=F32)
                + lax.dot_general(held_high, low, nt, preferred_element_type=F32)
            )
            q = jnp.concatenate([logq[...]] * (chunk * users // LANES), axis=1)
            p_high, p_low = split(jnp.exp(score - q - lse))
            acc[...] += (
                jnp.dot(p_high, high, preferred_element_type=F32)
                + jnp.dot(p_low, high, preferred_element_type=F32)
                + jnp.dot(p_high, low, preferred_element_type=F32)
            )
            return carry

        lax.fori_loop(0, shards // chunk, over_users, 0)

        def put(j, carry):
            ids = [jnp.minimum(id_ref[base + j * 8 + k], rows - 1) for k in range(8)]
            added = [acc[pl.ds(j * 8 + k, 1), :] for k in range(8)]
            for row, x in zip(ids, added, strict=True):
                out_ref[pl.ds(row, 1), :] = out_ref[pl.ds(row, 1), :] + x
            return carry

        lax.fori_loop(0, block // 8, put, 0)
        return carry

    lax.fori_loop(0, (count + block - 1) // block, add_block, 0)


def output_rows(users, block, cap_pos, scalars, lse, near, far, table):
    rows, width = table.shape
    shards = lse.shape[0]
    return pl.pallas_call(
        functools.partial(output_kernel, users, block, cap_pos),
        out_shape=jax.ShapeDtypeStruct((rows, width), F32),
        in_specs=[pl.BlockSpec(memory_space=pltpu.SMEM)] * len(scalars)
        + [pl.BlockSpec(memory_space=pltpu.VMEM)]
        + [pl.BlockSpec(memory_space=pltpu.HBM)] * 3,
        out_specs=pl.BlockSpec(memory_space=pltpu.VMEM),
        scratch_shapes=[
            pltpu.VMEM((block, width), F32),
            pltpu.VMEM((block, LANES), F32),
            pltpu.VMEM((block, width), F32),
            pltpu.VMEM((shards, users, width), F32),
            pltpu.VMEM(table.shape, F32),
            pltpu.SemaphoreType.DMA((3,)),
        ],
        compiler_params=pltpu.CompilerParams(vmem_limit_bytes=62 << 20),
        cost_estimate=pl.CostEstimate(flops=0, bytes_accessed=40 << 20, transcendentals=0),
    )(*scalars, lse, near, far, table)


def shard_counts(owners, shards):
    return jnp.sum((owners[:, None] == jnp.arange(shards, dtype=I32)[None, :]).astype(I32), axis=0)


def fill_owners(owners, shards, cap):
    lack = cap - shard_counts(owners, shards)
    ends = jnp.sum(jnp.where(jnp.tri(shards, dtype=jnp.bool_), lack[None, :], 0), axis=1)
    extra = jnp.arange(shards * cap - owners.shape[0], dtype=I32)
    return jnp.sum((extra[:, None] >= ends[None, :]).astype(I32), axis=1)


def request_keys(table, ids, used, user, users, rows, shards, cap):
    owner = lax.div(ids, I32(rows))
    unit = rows * users
    real = ((table * shards + owner) * 2 + (1 - used)) * unit + lax.rem(ids, I32(rows)) * users + user
    extra = ((table * shards + fill_owners(owner, shards, cap)) * 2 + 1) * unit
    return [real, extra]


def decode_keys(keys, users, rows):
    used = lax.rem(lax.div(keys, I32(rows * users)), I32(2)) == 0
    row = lax.rem(lax.div(keys, I32(users)), I32(rows))
    return jnp.where(used, row, rows), jnp.where(used, lax.rem(keys, I32(users)), 0)


def body(
    watch_ids,
    watch_len,
    search_ids,
    search_len,
    search_mask,
    positive_ids,
    logq_pos,
    negative_ids,
    logq_neg,
    dense_feats,
    watch_table,
    search_table,
    out_table,
    weight_one,
    bias_one,
    weight_two,
    bias_two,
    weight_three,
    bias_three,
):
    shards = lax.axis_size(AXES)
    n_tp = lax.axis_size("tp")
    n_dp = shards // n_tp
    mine = lax.axis_index(AXES)
    tp = lax.axis_index("tp")
    dp = lax.axis_index("dp")
    bits = shards.bit_length() - 1
    tp_bits = n_tp.bit_length() - 1
    rows, width = watch_table.shape
    users, bag = watch_ids.shape
    negs = negative_ids.shape[0]
    cap = max(2, 3 * users * bag // (2 * shards))
    cap_pos = max(2, 3 * users // (2 * shards))
    cap_pad = -(-cap // UNROLL) * UNROLL
    order_a = list(range(bits))
    order_b = [0, 2, 1] + list(range(3, bits))
    place_a, place_b = places(order_a), places(order_b)
    me = mine.astype(I32).reshape(1)

    n_feats, cols_two = weight_one.shape[0], weight_two.shape[1]
    biases = jnp.stack([bias_one, jnp.pad(bias_two, (0, width - cols_two))])
    biases = jnp.pad(biases, ((0, 6), (0, 0)))
    side_bit = tp_bits - 1
    deep = weight_two.shape[0] // 2

    slot = jnp.arange(users * bag, dtype=I32)
    slot_user = lax.div(slot, I32(bag))
    spot = jnp.arange(bag, dtype=I32)[None, :]
    watch_used = (spot < watch_len[:, None]).astype(I32).reshape(-1)
    search_used = ((spot < search_len[:, None]) & (search_mask[:, None] > 0)).astype(I32).reshape(-1)
    user_index = jnp.arange(users, dtype=I32)
    keys = jnp.concatenate(
        request_keys(0, watch_ids.reshape(-1), watch_used, slot_user, users, rows, shards, cap)
        + request_keys(1, search_ids.reshape(-1), search_used, slot_user, users, rows, shards, cap)
        + request_keys(2, positive_ids, 1, user_index, users, rows, shards, cap_pos)
    )
    keys = lax.sort(keys)
    ends = [shards * cap, 2 * shards * cap, shards * (2 * cap + cap_pos)]
    parts = [
        keys[: ends[0]].reshape(shards, cap),
        keys[ends[0] : ends[1]].reshape(shards, cap),
        keys[ends[1] : ends[2]].reshape(shards, cap_pos),
    ]
    decoded = [piece for part in parts for piece in decode_keys(part, users, rows)]
    request = jnp.concatenate(decoded, axis=1)
    my_pos_user = jnp.where(decoded[4] < rows, decoded[5], -1)
    neg_owner = lax.div(negative_ids, I32(rows))
    neg_local = lax.rem(negative_ids, I32(rows))
    neg_span = 1 << (negs - 1).bit_length()
    mean = negs / shards
    block = min(-(-negs // 8) * 8, max(8, int(mean + 4.2 * mean**0.5) // 8 * 8))
    neg_mine = neg_owner == mine
    neg_keys = jnp.where(neg_mine, neg_local, rows) * neg_span + jnp.arange(negs, dtype=I32)
    moved_one, request = exchange([(weight_one, side_bit)], shards, [request.reshape(shards, 1, -1)])
    request, neg_keys = lax.optimization_barrier((request, neg_keys))
    asked = lax.all_to_all(request, AXES, split_axis=0, concat_axis=0, tiled=True)
    moved_two, moved_bias, asked, neg_keys = exchange(
        [(weight_two, side_bit), (biases, side_bit)], shards, [asked, lax.sort(neg_keys)]
    )
    asked = asked.reshape(shards, -1)
    pos_row = asked[:, 4 * cap : 4 * cap + cap_pos]
    pos_user = asked[:, 4 * cap + cap_pos :]

    def prepared(start):
        row = asked[:, start : start + cap]
        user = asked[:, start + cap : start + 2 * cap]
        counts = jnp.sum((row < rows).astype(I32), axis=1)
        packed = 2 * row * (1 << SHIFT) + 2 * user
        packed = jnp.pad(packed, ((0, 0), (0, cap_pad - cap)), constant_values=2 * rows << SHIFT)
        return counts, packed.reshape(-1)

    watch_plan, search_plan = prepared(0), prepared(2 * cap)

    send, watch_keep = pool(place_a, users, cap_pad, me, *watch_plan, watch_table)
    send, search_counts = lax.optimization_barrier((send, search_plan[0]))
    search_send, search_keep = pool(place_b, users, cap_pad, me, search_counts, search_plan[1], search_table)
    watch_got, search_send, search_keep = exchange([(send, order_a[0])], shards, [search_send, search_keep])
    (search_got,) = exchange([(search_send, order_b[0])], shards)

    def cut(keep, got):
        half = keep.shape[0] // 2
        return keep[:half] + got[:half], keep[half:] + got[half:]

    watch_keep, watch_move = cut(watch_keep, watch_got)
    search_keep, search_move = cut(search_keep, search_got)
    watch_move, search_move, neg_keys, pos_late, moved_one, moved_two, moved_bias, lens = lax.optimization_barrier(
        (watch_move, search_move, neg_keys, pos_row, moved_one, moved_two, moved_bias, (watch_len, search_len, search_mask))
    )
    served = out_table[jnp.minimum(pos_late, rows - 1)]
    fetched = lax.all_to_all(served, AXES, split_axis=0, concat_axis=0, tiled=True)
    own_rows_id = jnp.pad(lax.div(neg_keys, I32(neg_span)), (0, block), constant_values=rows)
    own_place = jnp.pad(lax.rem(neg_keys, I32(neg_span)), (0, block))
    first_id = own_rows_id[:block]
    first_logq = logq_neg[own_place[:block]]
    logq_rows = -(-block // (8 * width)) * 8
    payload = jnp.concatenate(
        [
            out_table[jnp.minimum(first_id, rows - 1)],
            jnp.pad(first_logq, (0, logq_rows * width - block)).reshape(logq_rows, width),
        ]
    )
    side = (mine >> side_bit) & 1
    side_order = [b for b in reversed(range(bits)) if b != side_bit]
    side_places = jnp.array(
        [sum(((p >> k) & 1) << b for k, b in enumerate(side_order)) for p in range(1 << len(side_order))], I32
    )
    (moved,) = exchange([(payload, side_order[0])], shards)
    watch_got, search_got, fetched, moved = exchange(
        [(watch_move, order_a[1]), (search_move, order_b[1])], shards, [fetched, moved]
    )

    def by_tp(shares, k):
        near, far = shares[k]
        size = near.shape[0] // 2
        out = []
        for t in range(n_tp):
            apart = tp ^ t
            at = (apart >> 1) * size
            pick = [lax.dynamic_slice_in_dim(x, at, size, 0) for x in (near, far)]
            out.append(jnp.where((apart & 1) == 0, pick[0], pick[1]))
        return out

    watch_scale = 1.0 / lens[0].astype(F32)[:, None]
    search_scale = lens[2].astype(F32)[:, None] / lens[1].astype(F32)[:, None]
    rows_in = jnp.concatenate([jnp.stack([logq_pos, watch_scale[:, 0], search_scale[:, 0]]), jnp.zeros((5, users), F32)])
    fetched = fetched.reshape(-1, width)
    pos_match = my_pos_user.reshape(-1)[None, :] == user_index[:, None]
    pos_slot = jnp.sum(
        jnp.where(pos_match, jnp.arange(shards * cap_pos, dtype=I32)[None, :], 0), axis=1
    )
    pos_rows = fetched[pos_slot]

    side_rows = jnp.concatenate([payload, moved])
    watch_keep, watch_move = cut(watch_keep, watch_got)
    search_keep, search_move = cut(search_keep, search_got)
    shares = [
        jnp.concatenate(pair)
        for pair in zip((weight_one, weight_two, biases), (moved_one, moved_two, moved_bias), strict=True)
    ]
    watch_got, search_got, moved, pos_rows, rows_in, *shares = exchange(
        [(watch_move, order_a[2]), (search_move, order_b[2]), (side_rows, side_order[1])],
        shards,
        [pos_rows, rows_in, *shares],
    )
    side_rows = jnp.concatenate([side_rows, moved])
    both = [watch_keep + watch_got, search_keep + search_got]
    side_parts = [side_rows]
    for i in range(3, bits):
        half = both[0].shape[0] // 2
        keep = jnp.concatenate([x[:half] for x in both])
        moves = [(jnp.concatenate([x[half:] for x in both]), order_a[i])]
        beside = []
        if i == 3:
            moves += [(x, b) for x in shares for b in range(side_bit)]
        elif i == 4:
            moves[0], shares = lax.optimization_barrier((moves[0][0], shares))
            moves[0] = (moves[0], order_a[i])
            bias_parts = by_tp(shares, 2)
            beside = [
                *(jnp.concatenate(by_tp(shares, k), axis=1) for k in range(2)),
                jnp.concatenate([x[0] for x in bias_parts]),
                jnp.concatenate([x[1, :cols_two] for x in bias_parts]),
            ]
        if i < bits - 2:
            got, *rest, moved = exchange(moves + [(side_rows, side_order[i - 1])], shards, beside)
            if i == 4:
                beside, moved = [*rest[1:], moved], rest[0]
            side_rows = jnp.concatenate([side_rows, moved])
            side_parts = [side_rows]
        else:
            middle = side_rows.shape[0] // 2
            part = side_rows[:middle] if i == bits - 2 else side_rows[middle:]
            got, *rest, moved = exchange(moves + [(part, side_order[-2])], shards, beside)
            if i == 4:
                beside, moved = [*rest[1:], moved], rest[0]
            side_parts.append(moved)
        if i == 3:
            shares = list(zip(shares, rest, strict=True))
        elif i == 4:
            w_one, w_two, b_one, b_two = beside
        total = keep + got
        both = [total[:half], total[half:]]
    side_rows = jnp.concatenate(side_parts)
    watch_sum, search_sum = both
    (side_got,) = exchange([(side_rows, side_order[-1])], shards)

    neg_parts = [side_rows, side_got]
    part_rows = side_rows.shape[0]
    owners_part = part_rows // payload.shape[0]
    neg_count = shard_counts(neg_owner, shards)
    neg_most = jnp.max(neg_count)
    side_count = neg_count[mine ^ side_places]

    def part_logq(part, counts):
        real = jnp.arange(block, dtype=I32)[None, :] < counts[:, None]
        logq = part.reshape(owners_part, -1, width)[:, block:, :].reshape(owners_part, -1)[:, :block]
        return jnp.pad(jnp.where(real, logq, BIG), ((0, 0), (0, logq_rows)), constant_values=BIG).reshape(-1)

    neg_logqs = [part_logq(x, side_count[k * owners_part : (k + 1) * owners_part]) for k, x in enumerate(neg_parts)]

    watch_sum = watch_sum.reshape(users, width)
    search_sum = search_sum.reshape(users, width)
    feats = jnp.concatenate([watch_sum * watch_scale, search_sum * search_scale, dense_feats], axis=1)

    def first_layer(x):
        return matmul(x, w_one) + b_one


    quarter = -(-negs // 4)
    assert quarter <= part_rows

    def all_negatives(state):
        local = jnp.where(neg_mine[:, None], out_table[neg_local], 0.0)
        for b in range(bits):
            local = local + swap(local, 1 << b, shards)
        full = jnp.pad(local, ((0, 4 * quarter - negs), (0, 0)))
        logq = jnp.pad(logq_neg, (0, 4 * quarter - negs), constant_values=BIG)
        starts = [(2 * side + k) * quarter for k in range(2)]
        more = part_rows - quarter
        return (
            jnp.zeros((), I32),
            *[jnp.pad(lax.dynamic_slice_in_dim(full, at, quarter), ((0, more), (0, 0))) for at in starts],
            *[jnp.pad(lax.dynamic_slice_in_dim(logq, at, quarter), (0, more), constant_values=BIG) for at in starts],
        )

    overflow = (neg_most > block).astype(I32)
    _, *neg_all = lax.while_loop(lambda state: state[0] > 0, all_negatives, (overflow, *neg_parts, *neg_logqs))
    neg_parts, neg_logqs = neg_all[:2], neg_all[2:]

    z_one = first_layer(feats)
    z_two = matmul(jax.nn.gelu(z_one), w_two) + b_two
    z_three = matmul(jax.nn.gelu(z_two), weight_three) + bias_three
    user_vec = jax.nn.gelu(z_three)

    (partner_vec,) = exchange([(user_vec, side_bit)], shards)
    far_bits = list(reversed(range(3, bits)))
    user_held, vec_held, feats_held = lax.optimization_barrier((user_vec, user_vec, feats))
    here = side_sums(vec_held, neg_parts, neg_logqs)
    user_got, feats_got, feats_sib, here, partner_vec = exchange(
        [(user_held, far_bits[0]), (feats_held, side_bit), (feats_held, 0)], shards, [here, partner_vec]
    )
    user_part = jnp.concatenate([user_vec, user_got])
    user_part, partner_vec, feats_got = lax.optimization_barrier((user_part, partner_vec, feats_got))
    sent = side_sums(partner_vec, neg_parts, neg_logqs)
    user_got, feats_far, sent = exchange([(user_part, far_bits[1]), (feats_got, 0)], shards, [sent])
    user_part = jnp.concatenate([user_part, user_got])
    for b in far_bits[2:]:
        (user_got,) = exchange([(user_part, b)], shards)
        user_part = jnp.concatenate([user_part, user_got])
    (there,) = exchange([(sent, side_bit)], shards)
    g_three, both, dense_grad, loss_sum = finish(
        n_feats, here, there, rows_in, user_vec, pos_rows, z_one, z_two, z_three, w_one, w_two, weight_three
    )

    rows_three = weight_three.shape[0] // n_tp
    used_rows = weight_one.shape[0] + deep + rows_three + 4
    n_rows = -(-used_rows // (8 * n_dp)) * 8 * n_dp
    dp_order = [*range(tp_bits + 1, bits), tp_bits]

    def halves(total, b):
        bit = (mine >> b) & 1
        half = total.shape[0] // 2
        return (
            lax.dynamic_slice_in_dim(total, bit * half, half, 0),
            lax.dynamic_slice_in_dim(total, (1 - bit) * half, half, 0),
        )

    def joined(total, other, b):
        bit = (mine >> b) & 1
        return jnp.concatenate([jnp.where(bit == 0, total, other), jnp.where(bit == 0, other, total)])

    def scatter(total, b):
        kept, moved = halves(total, b)
        return kept, (moved, b)

    both, g_three, user_part = lax.optimization_barrier((both, g_three, user_part))
    assert side_bit == 1
    user_order = [*far_bits, 1, 2, 0]
    apart = mine ^ jnp.arange(shards, dtype=I32)
    user_at = sum(((apart >> b) & 1) << k for k, b in enumerate(user_order))
    scalars = [
        jnp.sum(neg_mine.astype(I32)).reshape(1), own_rows_id, own_place, logq_neg, pos_row.reshape(-1),
        pos_user.reshape(-1), user_at,
    ]
    table_rows = 2 * users
    for i in reversed(range(1, bits)):
        if i > 2:
            moves = [(both, order_a[i])]
        elif i == 2:
            pairs = both.reshape(-1, 2 * table_rows + 8, LANES)
            watch_out, search_out = (
                pairs[:, k * table_rows : (k + 1) * table_rows].reshape(-1, LANES) for k in range(2)
            )
            stats = pairs[:, 2 * table_rows :].reshape(-1, LANES)
            moves = [(watch_out, order_a[i]), (search_out, order_b[i])]
        else:
            watch_out, search_out = jnp.concatenate(watch_pieces), jnp.concatenate(search_pieces)
            moves = [(watch_out, order_a[i]), (search_out, order_b[i])]
        if i == bits - 1:
            feats_group = jnp.concatenate([feats, feats_got, feats_sib, feats_far])
            z_one_group = first_layer(feats_group)
            z_two_group = matmul(jax.nn.gelu(z_one_group), w_two) + b_two
            *gots, user_x, user_y, g_got, z_one_group, z_two_group = exchange(
                moves + [(user_part, 1), (user_part, 2), (g_three, side_bit)], shards, [z_one_group, z_two_group]
            )
        elif i == bits - 2:
            both_held, user_held, g_held, z_two_group = lax.optimization_barrier(
                (both, user_x, (g_three, g_got), z_two_group)
            )
            g_group = jnp.concatenate([*g_held, *exchange([(x, 0) for x in g_held], shards)])
            total = weight_block(
                n_rows, tp.astype(I32).reshape(1), loss_sum[0, :1],
                feats_group, z_one_group, z_two_group, g_group, w_two, weight_three,
            )
            *gots, user_xy, total = exchange([(both_held, order_a[i]), (user_held, 2)], shards, [total])
            kept, move = scatter(total, dp_order[0])
            done = 1
        elif i > 1:
            beside = []
            if i == 2:
                held = lax.optimization_barrier((*(x for x, _ in moves), move[0], stats, (user_part, user_x, user_y, user_xy)))
                moves = [(x, y[1]) for x, y in zip(held[:2], moves, strict=True)]
                move, stats = (held[2], move[1]), held[3]
                stats = jnp.concatenate([stats, *exchange([(stats, 1), (stats, 2), (stats, 1, 2)], shards)])
                user_near = jnp.concatenate(held[4])
                user_far, stats_far = exchange([(user_near, 0), (stats, 0)], shards)
                stats = jnp.concatenate([stats, stats_far]).reshape(shards, 8, LANES)
                beside = [user_near, user_far, stats, stats[:, 1].reshape(-1), scalars]
            *gots, got, user_near, user_far, stats, coefs, scalars = exchange(moves + [move], shards, beside) if beside else (
                *exchange(moves + [move], shards), None, None, None, None, scalars
            )
            kept, move = scatter(kept + got, dp_order[done])
            done += 1
        else:
            watch_out, search_out, first, user_near = lax.optimization_barrier(
                (watch_out, search_out, move[0], user_near)
            )
            output_grad = output_rows(
                users, block, cap_pos, [*scalars, coefs], stats,
                *[x.reshape(shards // 2, users, width) for x in (user_near, user_far)], out_table,
            )
            *gots, got, output_grad = exchange(
                [(watch_out, order_a[i]), (search_out, order_b[i]), (first, move[1])], shards, [output_grad]
            )
            kept, move = scatter(kept + got, dp_order[done])
        if i > 2:
            both = jnp.concatenate([both, *gots])
        else:
            watch_pieces, search_pieces = [watch_out, gots[0]], [search_out, gots[1]]

    *far, got = exchange(
        [(x, order_a[0]) for x in watch_pieces] + [(x, order_b[0]) for x in search_pieces] + [move], shards
    )
    watch_pieces, search_pieces = watch_pieces + far[:2], search_pieces + far[2:]
    total = kept + got
    for b in reversed(dp_order[2:]):
        (got,) = exchange([(total, b)], shards)
        total = joined(total, got, b)
    watch_counts, total = lax.optimization_barrier((watch_plan[0], total))
    watch_grad = spread(place_a, users, cap_pad, rows, me, watch_counts, watch_plan[1], *watch_pieces)
    got, watch_grad = exchange([(total, dp_order[1])], shards, [watch_grad])
    total = joined(total, got, dp_order[1])

    search_counts, total = lax.optimization_barrier((search_plan[0], total))
    search_grad = spread(place_b, users, cap_pad, rows, me, search_counts, search_plan[1], *search_pieces)
    got, search_grad = exchange([(total, dp_order[0])], shards, [search_grad])
    total = joined(total, got, dp_order[0])

    at = weight_one.shape[0]
    w_one_grad = total[:at]
    w_two_grad = jnp.concatenate([total[at : at + deep, :cols_two], total[at : at + deep, cols_two:]])
    at += deep
    b_one_grad = total[at + rows_three]
    b_two_grad = total[at + rows_three + 1, :cols_two]
    b_three_grad = total[at + rows_three + 2]
    whole = total[at : at + rows_three + 8]
    others = exchange([(whole, *[b for b in range(tp_bits) if r >> b & 1]) for r in range(1, n_tp)], shards)
    whole = jnp.stack([whole, *others])
    whole = jnp.concatenate([lax.dynamic_slice_in_dim(whole, t ^ tp, 1, 0) for t in range(n_tp)])
    w_three_grad = whole[:, :rows_three].reshape(-1, width)
    mean_loss = jnp.sum(whole[:, rows_three + 3, 0]) / F32(users * shards)
    return (
        mean_loss,
        watch_grad,
        search_grad,
        output_grad,
        w_one_grad,
        b_one_grad,
        w_two_grad,
        b_two_grad,
        w_three_grad,
        b_three_grad,
        dense_grad,
    )


def solution(mesh):
    both = P(AXES)
    rows = P(AXES, None)
    in_specs = (
        rows, both, rows, both, both, both, both, P(), P(), rows, rows, rows, rows,
        P(None, "tp"), P("tp"), P(None, "tp"), P("tp"), P(), P(),
    )
    out_specs = (
        P(), rows, rows, rows, P(None, "tp"), P("tp"), P(None, "tp"), P("tp"), P(), P(), rows,
    )
    return jax.shard_map(body, mesh=mesh, in_specs=in_specs, out_specs=out_specs, check_vma=False)
```

```python
import functools

import jax
import jax.numpy as jnp
from jax import lax
from jax.experimental import pallas as pl
from jax.experimental.pallas import tpu as pltpu
from jax.sharding import PartitionSpec as P

AXES = ("dp", "tp")
F32 = jnp.float32
I32 = jnp.int32
BIG = 1e30
LANES = 128
GROUP = 4
UNROLL = 8
SHIFT = 9
PAD_ROWS = 8
PARTS = 4
PIECES = 4


def matmul(left, right):
    return jnp.dot(left, right, precision=lax.Precision.HIGH, preferred_element_type=F32)


def matmul_t(left, right):
    return lax.dot_general(
        left, right, (((1,), (1,)), ((), ())), precision=lax.Precision.HIGH, preferred_element_type=F32
    )


def inner_rows(left, right):
    return lax.dot_general(
        left, right, (((0,), (0,)), ((), ())), precision=lax.Precision.HIGH, preferred_element_type=F32
    )


def swap(x, mask, shards):
    return lax.ppermute(x, AXES, [(i, i ^ mask) for i in range(shards)])


def after(x, *earlier):
    return lax.optimization_barrier((x, *earlier))[0]


def exchange(moves, shards, beside=()):
    held = lax.optimization_barrier(tuple(x for x, *_ in moves))
    got = tuple(swap(x, sum(1 << b for b in move[1:]), shards) for x, move in zip(held, moves, strict=True))
    return lax.optimization_barrier(got + tuple(beside))


def places(order):
    n = len(order)
    return [sum(((p >> (n - 1 - j)) & 1) << order[j] for j in range(n)) for p in range(1 << n)]


def group_bounds(me_ref, cnt_ref, members, cap):
    owners = [me_ref[0] ^ q for q in members]
    most = cnt_ref[owners[0]]
    for owner in owners[1:]:
        most = jnp.maximum(most, cnt_ref[owner])
    return [owner * cap for owner in owners], (most + UNROLL - 1) // UNROLL


def pool_kernel(places, users, cap, me_ref, cnt_ref, idx_ref, tab_ref, send_ref, keep_ref, tab, raw, sems):
    rows = tab_ref.shape[0]
    part = rows // PARTS
    copies = [
        pltpu.make_async_copy(tab_ref.at[pl.ds(n * part, part)], raw.at[pl.ds(n * part, part)], sems.at[n])
        for n in range(PARTS)
    ]
    for copy in copies:
        copy.start()
    tab[pl.ds(2 * rows, 2 * PAD_ROWS), :] = jnp.zeros((2 * PAD_ROWS, LANES), F32)
    send_ref[...] = jnp.zeros_like(send_ref)
    keep_ref[...] = jnp.zeros_like(keep_ref)
    for n, copy in enumerate(copies):
        copy.wait()
        for h in range(2):
            tab[pl.ds(2 * n * part + h, part, 2), :] = raw[pl.ds(n * part, part), h * LANES : (h + 1) * LANES]
    half = len(places) // 2
    for start in range(0, len(places), GROUP):
        out = keep_ref if start < half else send_ref
        first = (start % half) * 2 * users
        bases, steps = group_bounds(me_ref, cnt_ref, places[start : start + GROUP], cap)

        def step(i, carry, out=out, first=first, bases=bases):
            picks = [[idx_ref[base + (i * UNROLL + u)] for base in bases] for u in range(UNROLL)]
            source = [[tab[pl.ds(pl.multiple_of(v >> SHIFT, 2), 2), :] for v in row] for row in picks]
            for u in range(UNROLL):
                where = [
                    pl.ds(pl.multiple_of(first + k * 2 * users + (v & ((1 << SHIFT) - 1)), 2), 2)
                    for k, v in enumerate(picks[u])
                ]
                held = [out[w, :] for w in where]
                for k in range(GROUP):
                    out[where[k], :] = held[k] + source[u][k]
            return carry

        lax.fori_loop(0, steps, step, 0)


def pool(places, users, cap, me, counts, index, table):
    rows, width = table.shape
    shards = len(places)
    return pl.pallas_call(
        functools.partial(pool_kernel, places, users, cap),
        out_shape=[jax.ShapeDtypeStruct((shards * users, LANES), F32)] * 2,
        in_specs=[pl.BlockSpec(memory_space=pltpu.SMEM)] * 3 + [pl.BlockSpec(memory_space=pltpu.HBM)],
        out_specs=[pl.BlockSpec(memory_space=pltpu.VMEM)] * 2,
        scratch_shapes=[
            pltpu.VMEM((2 * (rows + PAD_ROWS), LANES), F32),
            pltpu.VMEM((rows, width), F32),
            pltpu.SemaphoreType.DMA((PARTS,)),
        ],
        compiler_params=pltpu.CompilerParams(vmem_limit_bytes=62 << 20),
        cost_estimate=pl.CostEstimate(flops=0, bytes_accessed=40 << 20, transcendentals=0),
    )(me, counts, index, table)


def spread_kernel(places, users, cap, me_ref, cnt_ref, idx_ref, *refs):
    sources, out_ref, accs = refs[:PIECES], refs[PIECES], refs[PIECES + 1 :]
    rows = out_ref.shape[0]
    for acc in accs:
        acc[...] = jnp.zeros_like(acc)
    piece = len(places) // PIECES
    for start in range(0, len(places), GROUP):
        source_ref = sources[start // piece]
        first = (start % piece) * 2 * users
        bases, steps = group_bounds(me_ref, cnt_ref, places[start : start + GROUP], cap)

        def step(i, carry, source_ref=source_ref, first=first, bases=bases):
            picks = [[idx_ref[base + (i * UNROLL + u)] for base in bases] for u in range(UNROLL)]
            source = [
                [
                    source_ref[pl.ds(pl.multiple_of(first + k * 2 * users + (v & ((1 << SHIFT) - 1)), 2), 2), :]
                    for k, v in enumerate(row)
                ]
                for row in picks
            ]
            for u in range(UNROLL):
                for k in range(0, GROUP, len(accs)):
                    where = [pl.ds(pl.multiple_of(v >> SHIFT, 2), 2) for v in picks[u][k : k + len(accs)]]
                    held = [acc[w, :] for acc, w in zip(accs, where, strict=True)]
                    for n, acc in enumerate(accs):
                        acc[where[n], :] = held[n] + source[u][k + n]
            return carry

        lax.fori_loop(0, steps, step, 0)
    for h in range(2):
        out_ref[:, h * LANES : (h + 1) * LANES] = sum(acc[pl.ds(h, rows, 2), :] for acc in accs)


def spread(places, users, cap, rows, me, counts, index, *sources):
    width = 2 * LANES
    size = 4 * width * (3 * rows + 2 * sources[0].shape[0])
    return pl.pallas_call(
        functools.partial(spread_kernel, places, users, cap),
        out_shape=jax.ShapeDtypeStruct((rows, width), F32),
        in_specs=[pl.BlockSpec(memory_space=pltpu.SMEM)] * 3 + [pl.BlockSpec(memory_space=pltpu.VMEM)] * PIECES,
        out_specs=pl.BlockSpec(memory_space=pltpu.VMEM),
        scratch_shapes=[pltpu.VMEM((2 * (rows + PAD_ROWS), LANES), F32)] * 2,
        compiler_params=pltpu.CompilerParams(vmem_limit_bytes=size + (4 << 20)),
        cost_estimate=pl.CostEstimate(flops=0, bytes_accessed=40 << 20, transcendentals=0),
    )(me, counts, index, *sources)


def split(x):
    high = x.astype(jnp.bfloat16)
    return high, (x - high.astype(F32)).astype(jnp.bfloat16)


NN = (((1,), (0,)), ((), ()))
NT = (((1,), (1,)), ((), ()))


def product(left, right, dims):
    (l_high, l_low), (r_high, r_low) = left, right
    one = functools.partial(lax.dot_general, dimension_numbers=dims, preferred_element_type=F32)
    return one(l_high, r_high) + one(l_low, r_high) + one(l_high, r_low)


def down(row):
    return jnp.broadcast_to(row, (LANES, row.shape[1])).T


def side_kernel(vec_ref, *refs):
    out_ref = refs[-1]
    count = (len(refs) - 1) // 2
    parts = [split(r[...]) for r in refs[:count]]
    vectors = split(vec_ref[...])
    scores = [product(vectors, part, NT) - q[...] for part, q in zip(parts, refs[count:-1], strict=True)]
    top = functools.reduce(jnp.maximum, [jnp.max(x, axis=1, keepdims=True) for x in scores])
    weights = [jnp.exp(x - top) for x in scores]
    users, width = vec_ref.shape
    out_ref[:users, :] = sum(product(split(x), part, NN) for x, part in zip(weights, parts, strict=True))
    total = sum(jnp.sum(x, axis=1, keepdims=True) for x in weights)
    across = [jnp.broadcast_to(x, (users, LANES)).T[:8] for x in (top, total)]
    out_ref[users:, :] = jnp.concatenate(across, axis=1)


def side_sums(vectors, parts, logqs):
    users, width = vectors.shape
    return pl.pallas_call(
        side_kernel,
        out_shape=jax.ShapeDtypeStruct((users + 8, width), F32),
        in_specs=[pl.BlockSpec(memory_space=pltpu.VMEM)] * (1 + 2 * len(parts)),
        out_specs=pl.BlockSpec(memory_space=pltpu.VMEM),
        compiler_params=pltpu.CompilerParams(vmem_limit_bytes=32 << 20),
        cost_estimate=pl.CostEstimate(flops=0, bytes_accessed=16 << 20, transcendentals=0),
    )(vectors, *parts, *[q[None, :] for q in logqs])


def gelu(x):
    scale = (2.0 / jnp.pi) ** 0.5
    return 0.5 * x * (1.0 + jnp.tanh(scale * (x + 0.044715 * x * x * x)))


def gelu_slope(x):
    scale = (2.0 / jnp.pi) ** 0.5
    t = jnp.tanh(scale * (x + 0.044715 * x * x * x))
    return 0.5 * (1.0 + t) + 0.5 * x * (1.0 - t * t) * (scale * (1.0 + 3 * 0.044715 * x * x))


def finish_kernel(
    here_ref, there_ref, rows_ref, vec_ref, pos_ref, z1_ref, z2_ref, z3_ref, w1_ref, w2_ref, w3_ref,
    g3_ref, both_ref, dense_ref, loss_ref,
):
    users, width = vec_ref.shape
    halves = [slice(h * LANES, (h + 1) * LANES) for h in range(width // LANES)]
    top_here, sum_here = (down(here_ref[users : users + 1, h]) for h in halves)
    top_there, sum_there = (down(there_ref[users : users + 1, h]) for h in halves)
    logq, watch_scale, search_scale = (down(rows_ref[k : k + 1, :]) for k in range(3))
    s_pos = jnp.sum(vec_ref[...] * pos_ref[...], axis=1, keepdims=True) - logq
    top = jnp.maximum(jnp.maximum(top_here, top_there), s_pos)
    e_here, e_there, e_pos = jnp.exp(top_here - top), jnp.exp(top_there - top), jnp.exp(s_pos - top)
    totals = sum_here * e_here + sum_there * e_there + e_pos
    lse = top + jnp.log(totals)
    coef = e_pos / totals - 1.0
    e_here, e_there = e_here / totals, e_there / totals
    g_user = jnp.concatenate(
        [here_ref[:users, h] * e_here + there_ref[:users, h] * e_there + pos_ref[:, h] * coef for h in halves], axis=1
    )
    loss_ref[...] = jnp.broadcast_to(jnp.sum((lse - s_pos)[:, :1], axis=0, keepdims=True), loss_ref.shape)
    both_ref[4 * users :, :] = jnp.concatenate([lse.T[:1], coef.T[:1], jnp.zeros((6, LANES), F32)])
    g3 = g_user * gelu_slope(z3_ref[...])
    g2 = product(split(g3), split(w3_ref[...]), NT) * gelu_slope(z2_ref[...])
    g1 = product(split(g2), split(w2_ref[...]), NT) * gelu_slope(z1_ref[...])
    g0 = product(split(g1), split(w1_ref[...]), NT)
    g3_ref[...] = g3
    for k, scale in enumerate((watch_scale, search_scale)):
        for h in range(2):
            lanes = slice(k * width + h * LANES, k * width + (h + 1) * LANES)
            both_ref[pl.ds(2 * k * users + h, users, 2), :] = g0[:, lanes] * scale
    dense_ref[...] = g0[:, 2 * width :]


def finish(n_feats, *arrays):
    users, width = arrays[3].shape
    shapes = [(users, width), (4 * users + 8, LANES), (users, n_feats - 2 * width), (8, LANES)]
    return pl.pallas_call(
        finish_kernel,
        out_shape=[jax.ShapeDtypeStruct(x, F32) for x in shapes],
        in_specs=[pl.BlockSpec(memory_space=pltpu.VMEM)] * len(arrays),
        out_specs=[pl.BlockSpec(memory_space=pltpu.VMEM)] * len(shapes),
        compiler_params=pltpu.CompilerParams(vmem_limit_bytes=32 << 20),
        cost_estimate=pl.CostEstimate(flops=0, bytes_accessed=16 << 20, transcendentals=0),
    )(*arrays)


def hidden_kernel(x_ref, w1_ref, b1_ref, w2_ref, b2_ref, z1_ref, z2_ref):
    z1_ref[...] = product(split(x_ref[...]), split(w1_ref[...]), NN) + b1_ref[...]
    z2_ref[...] = product(split(gelu(z1_ref[...])), split(w2_ref[...]), NN) + b2_ref[...]


def hidden_layers(x, w1, b1, w2, b2):
    shapes = [jax.ShapeDtypeStruct((x.shape[0], w.shape[1]), F32) for w in (w1, w2)]
    return pl.pallas_call(
        hidden_kernel,
        out_shape=shapes,
        in_specs=[pl.BlockSpec(memory_space=pltpu.VMEM)] * 5,
        out_specs=[pl.BlockSpec(memory_space=pltpu.VMEM)] * 2,
        compiler_params=pltpu.CompilerParams(vmem_limit_bytes=32 << 20),
        cost_estimate=pl.CostEstimate(flops=0, bytes_accessed=24 << 20, transcendentals=0),
    )(x, w1, b1[None, :], w2, b2[None, :])


def weight_kernel(tp_ref, loss_ref, *refs):
    count = (len(refs) - 3) // 2
    out_ref, held, g2_ref, sems = refs[count], refs[count + 1 : -2], refs[-2], refs[-1]
    copies = [pltpu.make_async_copy(refs[n], held[n], sems.at[n]) for n in range(count)]
    for copy in copies:
        copy.start()
    for copy in copies:
        copy.wait()
    feats, z1, z2, g3, w2, w3 = held
    width = out_ref.shape[1]
    n_feats, n_deep = feats.shape[1], z1.shape[1] // 2
    n_tp = z1.shape[1] // width
    cols_two = z2.shape[1] // n_tp
    mine_one = pl.ds(pl.multiple_of(tp_ref[0] * width, LANES), width)
    mine_two = pl.ds(pl.multiple_of(tp_ref[0] * cols_two, LANES), cols_two)

    def turned(x):
        return split(x.T)

    three = split(g3[...])
    g2_ref[...] = product(three, split(w3[...]), NT) * gelu_slope(z2[...])
    two = g2_ref[:, mine_two]
    one = product(split(g2_ref[...]), split(w2[mine_one, :]), NT) * gelu_slope(z1[:, mine_one])
    out_ref[:n_feats, :] = product(turned(feats[...]), split(one), NN)
    for h in range(2):
        out_ref[n_feats : n_feats + n_deep, h * cols_two : (h + 1) * cols_two] = product(
            turned(gelu(z1[:, h * n_deep : (h + 1) * n_deep])), split(two), NN
        )
    at = n_feats + n_deep
    out_ref[at : at + cols_two, :] = product(turned(gelu(z2[:, mine_two])), three, NN)
    at += cols_two
    rest = out_ref.shape[0] - at
    out_ref[at:, :] = jnp.concatenate(
        [
            jnp.sum(one, axis=0, keepdims=True),
            jnp.concatenate([jnp.sum(two, axis=0, keepdims=True), jnp.zeros((1, width - cols_two), F32)], axis=1),
            jnp.sum(g3[...], axis=0, keepdims=True),
            jnp.full((1, width), loss_ref[0], F32),
            jnp.zeros((rest - 4, width), F32),
        ]
    )


def weight_block(n_rows, tp, loss, *arrays):
    width = arrays[3].shape[1]
    return pl.pallas_call(
        weight_kernel,
        out_shape=jax.ShapeDtypeStruct((n_rows, width), F32),
        in_specs=[pl.BlockSpec(memory_space=pltpu.SMEM)] * 2 + [pl.BlockSpec(memory_space=pltpu.HBM)] * len(arrays),
        out_specs=pl.BlockSpec(memory_space=pltpu.VMEM),
        scratch_shapes=[pltpu.VMEM(x.shape, F32) for x in (*arrays, arrays[2])]
        + [pltpu.SemaphoreType.DMA((len(arrays),))],
        compiler_params=pltpu.CompilerParams(vmem_limit_bytes=62 << 20),
        cost_estimate=pl.CostEstimate(flops=0, bytes_accessed=16 << 20, transcendentals=0),
    )(tp, loss, *arrays)


def output_kernel(
    users, block, cap_pos, cnt_ref, id_ref, place_ref, logq_ref, pos_ref, pos_user_ref, user_at, coef_at, lse_at, coef_ref, lse_ref,
    *refs,
):
    user_hbm, tab_hbm = refs[:8], refs[8]
    out_ref, held, logq, acc, user_ref, tab_ref, sems = refs[9:]
    rows = out_ref.shape[0]
    shards = user_ref.shape[0]
    chunk = 4
    tab_copy = pltpu.make_async_copy(tab_hbm, tab_ref, sems.at[0])
    piece = shards // len(user_hbm)
    user_copies = [
        pltpu.make_async_copy(x, user_ref.at[pl.ds(n * piece, piece)], sems.at[1 + n]) for n, x in enumerate(user_hbm)
    ]
    for copy in user_copies:
        copy.start()
    tab_copy.start()
    out_ref[...] = jnp.zeros_like(out_ref)
    for copy in user_copies:
        copy.wait()

    def add_pos(s, carry):
        entries = [(pos_ref[s * cap_pos + k], pos_user_ref[s * cap_pos + k]) for k in range(cap_pos)]
        coefs = [jnp.where(row < rows, coef_ref[coef_at[s] * users + user], 0.0) for row, user in entries]
        added = [user_ref[user_at[s], pl.ds(user, 1), :] * c for (_, user), c in zip(entries, coefs, strict=True)]
        for (row, _), x in zip(entries, added, strict=True):
            at = pl.ds(jnp.minimum(row, rows - 1), 1)
            out_ref[at, :] = out_ref[at, :] + x
        return carry

    lax.fori_loop(0, shards, add_pos, 0)
    tab_copy.wait()
    count = cnt_ref[0]

    def add_block(r, carry):
        base = r * block

        def fetch(k, carry):
            row = id_ref[base + k]
            held[pl.ds(k, 1), :] = tab_ref[pl.ds(jnp.minimum(row, rows - 1), 1), :]
            q = jnp.where(row < rows, logq_ref[place_ref[base + k]], F32(BIG))
            logq[pl.ds(k, 1), :] = jnp.full((1, LANES), q, F32)
            return carry

        lax.fori_loop(0, block, fetch, 0, unroll=8)
        acc[...] = jnp.zeros_like(acc)
        held_high, held_low = split(held[...])

        def over_users(c, carry):
            parts = [user_ref[c * chunk + j, :users, :] for j in range(chunk)]
            lse = jnp.concatenate(
                [lse_ref[lse_at[c * chunk + j], 0:1, :] for j in range(chunk)], axis=1
            )
            high, low = split(jnp.concatenate(parts))
            nt = (((1,), (1,)), ((), ()))
            score = (
                lax.dot_general(held_high, high, nt, preferred_element_type=F32)
                + lax.dot_general(held_low, high, nt, preferred_element_type=F32)
                + lax.dot_general(held_high, low, nt, preferred_element_type=F32)
            )
            q = jnp.concatenate([logq[...]] * (chunk * users // LANES), axis=1)
            p_high, p_low = split(jnp.exp(score - q - lse))
            acc[...] += (
                jnp.dot(p_high, high, preferred_element_type=F32)
                + jnp.dot(p_low, high, preferred_element_type=F32)
                + jnp.dot(p_high, low, preferred_element_type=F32)
            )
            return carry

        lax.fori_loop(0, shards // chunk, over_users, 0)

        def put(j, carry):
            ids = [jnp.minimum(id_ref[base + j * 8 + k], rows - 1) for k in range(8)]
            added = [acc[pl.ds(j * 8 + k, 1), :] for k in range(8)]
            for row, x in zip(ids, added, strict=True):
                out_ref[pl.ds(row, 1), :] = out_ref[pl.ds(row, 1), :] + x
            return carry

        lax.fori_loop(0, block // 8, put, 0)
        return carry

    lax.fori_loop(0, (count + block - 1) // block, add_block, 0)


def output_rows(users, block, cap_pos, scalars, lse, *arrays):
    table = arrays[-1]
    rows, width = table.shape
    shards = lse.shape[0]
    return pl.pallas_call(
        functools.partial(output_kernel, users, block, cap_pos),
        out_shape=jax.ShapeDtypeStruct((rows, width), F32),
        in_specs=[pl.BlockSpec(memory_space=pltpu.SMEM)] * len(scalars)
        + [pl.BlockSpec(memory_space=pltpu.VMEM)]
        + [pl.BlockSpec(memory_space=pltpu.HBM)] * len(arrays),
        out_specs=pl.BlockSpec(memory_space=pltpu.VMEM),
        scratch_shapes=[
            pltpu.VMEM((block, width), F32),
            pltpu.VMEM((block, LANES), F32),
            pltpu.VMEM((block, width), F32),
            pltpu.VMEM((shards, users, width), F32),
            pltpu.VMEM(table.shape, F32),
            pltpu.SemaphoreType.DMA((len(arrays),)),
        ],
        compiler_params=pltpu.CompilerParams(vmem_limit_bytes=62 << 20),
        cost_estimate=pl.CostEstimate(flops=0, bytes_accessed=40 << 20, transcendentals=0),
    )(*scalars, lse, *arrays)


def shard_counts(owners, shards):
    return jnp.sum((owners[:, None] == jnp.arange(shards, dtype=I32)[None, :]).astype(I32), axis=0)


def fill_owners(owners, shards, cap):
    lack = cap - shard_counts(owners, shards)
    ends = jnp.sum(jnp.where(jnp.tri(shards, dtype=jnp.bool_), lack[None, :], 0), axis=1)
    extra = jnp.arange(shards * cap - owners.shape[0], dtype=I32)
    return jnp.sum((extra[:, None] >= ends[None, :]).astype(I32), axis=1)


def request_keys(table, ids, used, user, users, rows, shards, cap):
    owner = lax.div(ids, I32(rows))
    unit = rows * users
    real = ((table * shards + owner) * 2 + (1 - used)) * unit + lax.rem(ids, I32(rows)) * users + user
    extra = ((table * shards + fill_owners(owner, shards, cap)) * 2 + 1) * unit
    return [real, extra]


def decode_keys(keys, users, rows):
    used = lax.rem(lax.div(keys, I32(rows * users)), I32(2)) == 0
    row = lax.rem(lax.div(keys, I32(users)), I32(rows))
    return jnp.where(used, row, rows), jnp.where(used, lax.rem(keys, I32(users)), 0)


def body(
    watch_ids,
    watch_len,
    search_ids,
    search_len,
    search_mask,
    positive_ids,
    logq_pos,
    negative_ids,
    logq_neg,
    dense_feats,
    watch_table,
    search_table,
    out_table,
    weight_one,
    bias_one,
    weight_two,
    bias_two,
    weight_three,
    bias_three,
):
    shards = lax.axis_size(AXES)
    n_tp = lax.axis_size("tp")
    n_dp = shards // n_tp
    mine = lax.axis_index(AXES)
    tp = lax.axis_index("tp")
    dp = lax.axis_index("dp")
    bits = shards.bit_length() - 1
    tp_bits = n_tp.bit_length() - 1
    rows, width = watch_table.shape
    users, bag = watch_ids.shape
    negs = negative_ids.shape[0]
    cap = max(2, 3 * users * bag // (2 * shards))
    cap_pos = max(2, 3 * users // (2 * shards))
    cap_pad = -(-cap // UNROLL) * UNROLL
    order_a = list(range(bits))
    order_b = [0, 2, 1] + list(range(3, bits))
    place_a, place_b = places(order_a), places(order_b)
    me = mine.astype(I32).reshape(1)

    n_feats, cols_two = weight_one.shape[0], weight_two.shape[1]
    biases = jnp.stack([bias_one, jnp.pad(bias_two, (0, width - cols_two))])
    biases = jnp.pad(biases, ((0, 6), (0, 0)))
    side_bit = tp_bits - 1
    deep = weight_two.shape[0] // 2

    slot = jnp.arange(users * bag, dtype=I32)
    slot_user = lax.div(slot, I32(bag))
    spot = jnp.arange(bag, dtype=I32)[None, :]
    watch_used = (spot < watch_len[:, None]).astype(I32).reshape(-1)
    search_used = ((spot < search_len[:, None]) & (search_mask[:, None] > 0)).astype(I32).reshape(-1)
    user_index = jnp.arange(users, dtype=I32)
    keys = jnp.concatenate(
        request_keys(0, watch_ids.reshape(-1), watch_used, slot_user, users, rows, shards, cap)
        + request_keys(1, search_ids.reshape(-1), search_used, slot_user, users, rows, shards, cap)
        + request_keys(2, positive_ids, 1, user_index, users, rows, shards, cap_pos)
    )
    keys = lax.sort(keys)
    ends = [shards * cap, 2 * shards * cap, shards * (2 * cap + cap_pos)]
    parts = [
        keys[: ends[0]].reshape(shards, cap),
        keys[ends[0] : ends[1]].reshape(shards, cap),
        keys[ends[1] : ends[2]].reshape(shards, cap_pos),
    ]
    decoded = [piece for part in parts for piece in decode_keys(part, users, rows)]
    request = jnp.concatenate(decoded, axis=1)
    my_pos_user = jnp.where(decoded[4] < rows, decoded[5], -1)
    neg_owner = lax.div(negative_ids, I32(rows))
    neg_local = lax.rem(negative_ids, I32(rows))
    neg_span = 1 << (negs - 1).bit_length()
    mean = negs / shards
    block = min(-(-negs // 8) * 8, max(8, int(mean + 4.2 * mean**0.5) // 8 * 8))
    neg_mine = neg_owner == mine
    neg_keys = jnp.where(neg_mine, neg_local, rows) * neg_span + jnp.arange(negs, dtype=I32)
    moved_one, request = exchange([(weight_one, side_bit)], shards, [request.reshape(shards, 1, -1)])
    request, neg_keys = lax.optimization_barrier((request, neg_keys))
    asked = lax.all_to_all(request, AXES, split_axis=0, concat_axis=0, tiled=True)
    moved_two, moved_bias, asked, neg_keys = exchange(
        [(weight_two, side_bit), (biases, side_bit)], shards, [asked, lax.sort(neg_keys)]
    )
    asked = asked.reshape(shards, -1)
    pos_row = asked[:, 4 * cap : 4 * cap + cap_pos]
    pos_user = asked[:, 4 * cap + cap_pos :]

    def prepared(start):
        row = asked[:, start : start + cap]
        user = asked[:, start + cap : start + 2 * cap]
        counts = jnp.sum((row < rows).astype(I32), axis=1)
        packed = 2 * row * (1 << SHIFT) + 2 * user
        packed = jnp.pad(packed, ((0, 0), (0, cap_pad - cap)), constant_values=2 * rows << SHIFT)
        return counts, packed.reshape(-1)

    watch_plan, search_plan = prepared(0), prepared(2 * cap)

    send, watch_keep = pool(place_a, users, cap_pad, me, *watch_plan, watch_table)
    send, search_counts = lax.optimization_barrier((send, search_plan[0]))
    search_send, search_keep = pool(place_b, users, cap_pad, me, search_counts, search_plan[1], search_table)
    watch_got, search_send, search_keep = exchange([(send, order_a[0])], shards, [search_send, search_keep])
    (search_got,) = exchange([(search_send, order_b[0])], shards)

    def cut(keep, got):
        half = keep.shape[0] // 2
        return keep[:half] + got[:half], keep[half:] + got[half:]

    watch_keep, watch_move = cut(watch_keep, watch_got)
    search_keep, search_move = cut(search_keep, search_got)
    watch_move, search_move, neg_keys, pos_late, moved_one, moved_two, moved_bias, lens = lax.optimization_barrier(
        (watch_move, search_move, neg_keys, pos_row, moved_one, moved_two, moved_bias, (watch_len, search_len, search_mask))
    )
    served = out_table[jnp.minimum(pos_late, rows - 1)]
    fetched = lax.all_to_all(served, AXES, split_axis=0, concat_axis=0, tiled=True)
    own_rows_id = jnp.pad(lax.div(neg_keys, I32(neg_span)), (0, block), constant_values=rows)
    own_place = jnp.pad(lax.rem(neg_keys, I32(neg_span)), (0, block))
    first_id = own_rows_id[:block]
    first_logq = logq_neg[own_place[:block]]
    logq_rows = -(-block // (8 * width)) * 8
    payload = jnp.concatenate(
        [
            out_table[jnp.minimum(first_id, rows - 1)],
            jnp.pad(first_logq, (0, logq_rows * width - block)).reshape(logq_rows, width),
        ]
    )
    side = (mine >> side_bit) & 1
    side_order = [b for b in reversed(range(bits)) if b != side_bit]
    side_places = jnp.array(
        [sum(((p >> k) & 1) << b for k, b in enumerate(side_order)) for p in range(1 << len(side_order))], I32
    )
    (moved,) = exchange([(payload, side_order[0])], shards)
    watch_got, search_got, fetched, moved = exchange(
        [(watch_move, order_a[1]), (search_move, order_b[1])], shards, [fetched, moved]
    )

    def by_tp(shares, k):
        near, far = shares[k]
        size = near.shape[0] // 2
        out = []
        for t in range(n_tp):
            apart = tp ^ t
            at = (apart >> 1) * size
            pick = [lax.dynamic_slice_in_dim(x, at, size, 0) for x in (near, far)]
            out.append(jnp.where((apart & 1) == 0, pick[0], pick[1]))
        return out

    watch_scale = 1.0 / lens[0].astype(F32)[:, None]
    search_scale = lens[2].astype(F32)[:, None] / lens[1].astype(F32)[:, None]
    rows_in = jnp.concatenate([jnp.stack([logq_pos, watch_scale[:, 0], search_scale[:, 0]]), jnp.zeros((5, users), F32)])
    fetched = fetched.reshape(-1, width)
    pos_match = my_pos_user.reshape(-1)[None, :] == user_index[:, None]
    pos_slot = jnp.sum(
        jnp.where(pos_match, jnp.arange(shards * cap_pos, dtype=I32)[None, :], 0), axis=1
    )
    pos_rows = fetched[pos_slot]

    side_rows = jnp.concatenate([payload, moved])
    watch_keep, watch_move = cut(watch_keep, watch_got)
    search_keep, search_move = cut(search_keep, search_got)
    shares = [
        jnp.concatenate(pair)
        for pair in zip((weight_one, weight_two, biases), (moved_one, moved_two, moved_bias), strict=True)
    ]
    watch_got, search_got, moved, pos_rows, rows_in, *shares = exchange(
        [(watch_move, order_a[2]), (search_move, order_b[2]), (side_rows, side_order[1])],
        shards,
        [pos_rows, rows_in, *shares],
    )
    side_rows = jnp.concatenate([side_rows, moved])
    both = [watch_keep + watch_got, search_keep + search_got]
    side_parts = [side_rows]
    for i in range(3, bits):
        half = both[0].shape[0] // 2
        keep = jnp.concatenate([x[:half] for x in both])
        moves = [(jnp.concatenate([x[half:] for x in both]), order_a[i])]
        beside = []
        if i == 3:
            moves += [(x, b) for x in shares for b in range(side_bit)]
        elif i == 4:
            moves[0], shares = lax.optimization_barrier((moves[0][0], shares))
            moves[0] = (moves[0], order_a[i])
            bias_parts = by_tp(shares, 2)
            beside = [
                *(jnp.concatenate(by_tp(shares, k), axis=1) for k in range(2)),
                jnp.concatenate([x[0] for x in bias_parts]),
                jnp.concatenate([x[1, :cols_two] for x in bias_parts]),
            ]
        if i < bits - 2:
            got, *rest, moved = exchange(moves + [(side_rows, side_order[i - 1])], shards, beside)
            if i == 4:
                beside, moved = [*rest[1:], moved], rest[0]
            side_rows = jnp.concatenate([side_rows, moved])
            side_parts = [side_rows]
        else:
            middle = side_rows.shape[0] // 2
            part = side_rows[:middle] if i == bits - 2 else side_rows[middle:]
            got, *rest, moved = exchange(moves + [(part, side_order[-2])], shards, beside)
            if i == 4:
                beside, moved = [*rest[1:], moved], rest[0]
            side_parts.append(moved)
        if i == 3:
            shares = list(zip(shares, rest, strict=True))
        elif i == 4:
            w_one, w_two, b_one, b_two = beside
        total = keep + got
        both = [total[:half], total[half:]]
    side_rows = jnp.concatenate(side_parts)
    watch_sum, search_sum = both
    (side_got,) = exchange([(side_rows, side_order[-1])], shards)

    neg_parts = [side_rows, side_got]
    part_rows = side_rows.shape[0]
    owners_part = part_rows // payload.shape[0]
    neg_count = shard_counts(neg_owner, shards)
    neg_most = jnp.max(neg_count)
    side_count = neg_count[mine ^ side_places]

    def part_logq(part, counts):
        real = jnp.arange(block, dtype=I32)[None, :] < counts[:, None]
        logq = part.reshape(owners_part, -1, width)[:, block:, :].reshape(owners_part, -1)[:, :block]
        return jnp.pad(jnp.where(real, logq, BIG), ((0, 0), (0, logq_rows)), constant_values=BIG).reshape(-1)

    neg_logqs = [part_logq(x, side_count[k * owners_part : (k + 1) * owners_part]) for k, x in enumerate(neg_parts)]

    watch_sum = watch_sum.reshape(users, width)
    search_sum = search_sum.reshape(users, width)
    feats = jnp.concatenate([watch_sum * watch_scale, search_sum * search_scale, dense_feats], axis=1)

    def first_layer(x):
        return matmul(x, w_one) + b_one


    quarter = -(-negs // 4)
    assert quarter <= part_rows

    def all_negatives(state):
        local = jnp.where(neg_mine[:, None], out_table[neg_local], 0.0)
        for b in range(bits):
            local = local + swap(local, 1 << b, shards)
        full = jnp.pad(local, ((0, 4 * quarter - negs), (0, 0)))
        logq = jnp.pad(logq_neg, (0, 4 * quarter - negs), constant_values=BIG)
        starts = [(2 * side + k) * quarter for k in range(2)]
        more = part_rows - quarter
        return (
            jnp.zeros((), I32),
            *[jnp.pad(lax.dynamic_slice_in_dim(full, at, quarter), ((0, more), (0, 0))) for at in starts],
            *[jnp.pad(lax.dynamic_slice_in_dim(logq, at, quarter), (0, more), constant_values=BIG) for at in starts],
        )

    overflow = (neg_most > block).astype(I32)
    _, *neg_all = lax.while_loop(lambda state: state[0] > 0, all_negatives, (overflow, *neg_parts, *neg_logqs))
    neg_parts, neg_logqs = neg_all[:2], neg_all[2:]

    z_one = first_layer(feats)
    z_two = matmul(jax.nn.gelu(z_one), w_two) + b_two
    z_three = matmul(jax.nn.gelu(z_two), weight_three) + bias_three
    user_vec = jax.nn.gelu(z_three)

    (partner_vec,) = exchange([(user_vec, side_bit)], shards)
    far_bits = list(reversed(range(3, bits)))
    user_held, vec_held, feats_held = lax.optimization_barrier((user_vec, user_vec, feats))
    here = side_sums(vec_held, neg_parts, neg_logqs)
    user_got, feats_got, feats_sib, here, partner_vec = exchange(
        [(user_held, far_bits[0]), (feats_held, side_bit), (feats_held, 0)], shards, [here, partner_vec]
    )
    user_part = jnp.concatenate([user_vec, user_got])
    user_part, partner_vec, feats_got = lax.optimization_barrier((user_part, partner_vec, feats_got))
    sent = side_sums(partner_vec, neg_parts, neg_logqs)
    user_got, feats_far, sent = exchange([(user_part, far_bits[1]), (feats_got, 0)], shards, [sent])
    user_part = jnp.concatenate([user_part, user_got])
    for b in far_bits[2:]:
        (user_got,) = exchange([(user_part, b)], shards)
        user_part = jnp.concatenate([user_part, user_got])
    (there,) = exchange([(sent, side_bit)], shards)
    g_three, both, dense_grad, loss_sum = finish(
        n_feats, here, there, rows_in, user_vec, pos_rows, z_one, z_two, z_three, w_one, w_two, weight_three
    )

    rows_three = weight_three.shape[0] // n_tp
    used_rows = weight_one.shape[0] + deep + rows_three + 4
    n_rows = -(-used_rows // (8 * n_dp)) * 8 * n_dp
    dp_order = [*range(tp_bits + 1, bits), tp_bits]

    def halves(total, b):
        bit = (mine >> b) & 1
        half = total.shape[0] // 2
        return (
            lax.dynamic_slice_in_dim(total, bit * half, half, 0),
            lax.dynamic_slice_in_dim(total, (1 - bit) * half, half, 0),
        )

    def joined(total, other, b):
        bit = (mine >> b) & 1
        return jnp.concatenate([jnp.where(bit == 0, total, other), jnp.where(bit == 0, other, total)])

    def scatter(total, b):
        kept, moved = halves(total, b)
        return kept, (moved, b)

    both, g_three, user_part = lax.optimization_barrier((both, g_three, user_part))
    assert side_bit == 1
    user_order = [*far_bits, 1, 2, 0]
    apart = mine ^ jnp.arange(shards, dtype=I32)
    user_at = sum(((apart >> b) & 1) << k for k, b in enumerate(user_order))
    stats_order = [*far_bits, 0, 1, 2]
    stats_at = sum(((apart >> b) & 1) << k for k, b in enumerate(stats_order))
    user_of = [sum(((p >> k) & 1) << b for k, b in enumerate(user_order)) for p in range(shards)]
    lse_at = [sum(((q >> b) & 1) << k for k, b in enumerate(stats_order)) for q in user_of]
    scalars = [
        jnp.sum(neg_mine.astype(I32)).reshape(1), own_rows_id, own_place, logq_neg, pos_row.reshape(-1),
        pos_user.reshape(-1), user_at, stats_at, jnp.array(lse_at, I32),
    ]
    table_rows = 2 * users
    for i in reversed(range(1, bits)):
        if i > 2:
            moves = [(both, order_a[i])]
        elif i == 2:
            pairs = both.reshape(-1, 2 * table_rows + 8, LANES)
            watch_out, search_out = (
                pairs[:, k * table_rows : (k + 1) * table_rows].reshape(-1, LANES) for k in range(2)
            )
            stats = pairs[:, 2 * table_rows :].reshape(-1, LANES)
            moves = [(watch_out, order_a[i]), (search_out, order_b[i])]
        else:
            watch_out, search_out = jnp.concatenate(watch_pieces), jnp.concatenate(search_pieces)
            moves = [(watch_out, order_a[i]), (search_out, order_b[i])]
        if i == bits - 1:
            feats_group = jnp.concatenate([feats, feats_got, feats_sib, feats_far])
            z_one_group, z_two_group = hidden_layers(feats_group, w_one, b_one, w_two, b_two)
            got, user_x, user_y, g_got, part_far, z_one_group, z_two_group = exchange(
                moves + [(user_part, 1), (user_part, 2), (g_three, side_bit), (user_part, 0)],
                shards,
                [z_one_group, z_two_group],
            )
            gots = [got]
        elif i == bits - 2:
            both_held, user_held, g_held, z_two_group = lax.optimization_barrier(
                (both, user_x, (g_three, g_got), z_two_group)
            )
            g_group = jnp.concatenate(g_held)
            g_group = jnp.concatenate([g_group, *exchange([(g_group, 0)], shards)])
            total = weight_block(
                n_rows, tp.astype(I32).reshape(1), loss_sum[0, :1],
                feats_group, z_one_group, z_two_group, g_group, w_two, weight_three,
            )
            got, user_xy, x_far, y_far, total = exchange(
                [(both_held, order_a[i]), (user_held, 2), (user_held, 0), (user_y, 0)], shards, [total]
            )
            gots = [got]
            kept, move = scatter(total, dp_order[0])
            done = 1
        elif i > 1:
            if i == 2:
                held = lax.optimization_barrier((*(x for x, _ in moves), move[0], user_xy, stats))
                stats = held[-1]
                for b in (0, 1, 2):
                    stats = jnp.concatenate([stats, *exchange([(stats, b)], shards)])
                stats = stats.reshape(shards, 8, LANES)
                *gots, got, xy_far, stats, coefs, scalars = exchange(
                    [(x, b) for x, (_, b) in zip(held[:3], [*moves, move], strict=True)] + [(held[3], 0)],
                    shards,
                    [stats, stats[:, 1].reshape(-1), scalars],
                )
                user_pieces = [user_part, user_x, user_y, user_xy, part_far, x_far, y_far, xy_far]
            else:
                *gots, got = exchange(moves + [move], shards)
            kept, move = scatter(kept + got, dp_order[done])
            done += 1
        else:
            watch_out, search_out, first, user_pieces = lax.optimization_barrier(
                (watch_out, search_out, move[0], user_pieces)
            )
            output_grad = output_rows(
                users, block, cap_pos, [*scalars, coefs], stats,
                *[x.reshape(-1, users, width) for x in user_pieces], out_table,
            )
            *gots, got, output_grad = exchange(
                [(watch_out, order_a[i]), (search_out, order_b[i]), (first, move[1])], shards, [output_grad]
            )
            kept, move = scatter(kept + got, dp_order[done])
        if i > 2:
            both = jnp.concatenate([both, *gots])
        else:
            watch_pieces, search_pieces = [watch_out, gots[0]], [search_out, gots[1]]

    *far, got = exchange(
        [(x, order_a[0]) for x in watch_pieces] + [(x, order_b[0]) for x in search_pieces] + [move], shards
    )
    watch_pieces, search_pieces = watch_pieces + far[:2], search_pieces + far[2:]
    total = kept + got
    for b in reversed(dp_order[2:]):
        (got,) = exchange([(total, b)], shards)
        total = joined(total, got, b)
    watch_counts, total = lax.optimization_barrier((watch_plan[0], total))
    watch_grad = spread(place_a, users, cap_pad, rows, me, watch_counts, watch_plan[1], *watch_pieces)
    got, watch_grad = exchange([(total, dp_order[1])], shards, [watch_grad])
    total = joined(total, got, dp_order[1])

    search_counts, total = lax.optimization_barrier((search_plan[0], total))
    search_grad = spread(place_b, users, cap_pad, rows, me, search_counts, search_plan[1], *search_pieces)
    got, search_grad = exchange([(total, dp_order[0])], shards, [search_grad])
    total = joined(total, got, dp_order[0])

    at = weight_one.shape[0]
    w_one_grad = total[:at]
    w_two_grad = jnp.concatenate([total[at : at + deep, :cols_two], total[at : at + deep, cols_two:]])
    at += deep
    b_one_grad = total[at + rows_three]
    b_two_grad = total[at + rows_three + 1, :cols_two]
    b_three_grad = total[at + rows_three + 2]
    whole = total[at : at + rows_three + 8]
    others = exchange([(whole, *[b for b in range(tp_bits) if r >> b & 1]) for r in range(1, n_tp)], shards)
    whole = jnp.stack([whole, *others])
    whole = jnp.concatenate([lax.dynamic_slice_in_dim(whole, t ^ tp, 1, 0) for t in range(n_tp)])
    w_three_grad = whole[:, :rows_three].reshape(-1, width)
    mean_loss = jnp.sum(whole[:, rows_three + 3, 0]) / F32(users * shards)
    return (
        mean_loss,
        watch_grad,
        search_grad,
        output_grad,
        w_one_grad,
        b_one_grad,
        w_two_grad,
        b_two_grad,
        w_three_grad,
        b_three_grad,
        dense_grad,
    )


def solution(mesh):
    both = P(AXES)
    rows = P(AXES, None)
    in_specs = (
        rows, both, rows, both, both, both, both, P(), P(), rows, rows, rows, rows,
        P(None, "tp"), P("tp"), P(None, "tp"), P("tp"), P(), P(),
    )
    out_specs = (
        P(), rows, rows, rows, P(None, "tp"), P("tp"), P(None, "tp"), P("tp"), P(), P(), rows,
    )
    return jax.shard_map(body, mesh=mesh, in_specs=in_specs, out_specs=out_specs, check_vma=False)
```
